32 devices in a mesh: ctx: 8 (over z, x), kvh: 4 (over y, core).
Axes of the slice: x: 2, y: 2, z: 4, core: 2. Of those that a mesh axis runs over, the one named last changes fastest.
Arguments:
- queries: bfloat16 [2048, 64, 128], P('ctx', 'kvh'), may hold values from -6 to 6
- keys: bfloat16 [2048, 8, 128], P(('ctx', 'kvh')), may hold values from -6 to 6
- values: bfloat16 [2048, 8, 128], P(('ctx', 'kvh')), may hold values from -6 to 6
- doc_blocks: int32 [4], replicated, may hold values from 1 to 6, 16 in all
Outputs:
- attended: bfloat16 [2048, 64, 128], P('ctx', 'kvh')
The draws below stay inside these ranges and needn't reach their ends.
Inputs may be any that keep to these rules, and one draw needn't show every extreme that they name: document i covers doc_blocks[i] * 128 tokens; the lengths sum to 2048 tokens.
All inputs are finite; a program needn't handle non-finite values.
Results may differ from the reference program's by a relative error of at most 0.004.
Values may be sent and summed in bfloat16 or wider, within the bound.
No kernel may reach another device: no remote copies, remote signals or barrier semaphores. Data moves between devices by JAX's collectives and lax.ppermute only.
A program may use at most 64 MiB of HBM per device.

```python
import math
import jax
import jax.numpy as jnp
import numpy as np
from jax import lax

QH = 64
KVH = 8
HD = 128
BLOCK = 128
TOK_DEV = 256
TOKENS = 2048
LOOK = 3
MAXBLK = 6
NDOCS = 4
N_CTX = 8


def rough_base(key, shape):
    first = jax.random.fold_in(key, 0)
    return jnp.clip(jax.random.normal(first, shape, jnp.float32), -6.0, 6.0)


def draw_queries(key, part):
    base = rough_base(jax.random.fold_in(key, 11), (TOKENS, QH, HD))
    return base.astype(jnp.bfloat16)


def draw_keys(key, part):
    base = rough_base(jax.random.fold_in(key, 13), (TOKENS, KVH, HD))
    return base.astype(jnp.bfloat16)


def steps_of(key, extent, cuts, low, largest):
    def one(dim, parts):
        steps = jax.random.uniform(jax.random.fold_in(jax.random.fold_in(key, 6), dim), (parts,), jnp.float32, low / len(cuts), largest / len(cuts))
        return jnp.repeat(jnp.exp(steps), extent[dim] // parts).reshape((-1,) + (1,) * (len(extent) - dim - 1))

    gain = one(*cuts[0])
    for cut in cuts[1:]:
        gain = gain * one(*cut)
    return gain


def profile(count, total, limit, slope):
    portions = [(1 << 20) // math.isqrt(grade ** slope) + 1 for grade in range(2, count + 1)]
    surplus, given = total - limit - (count - 1), [1] * (count - 1)
    while surplus > 0:
        candidates = [i for i in range(count - 1) if given[i] < limit]
        pool, remaining = sum([portions[i] for i in candidates]), surplus
        for i in candidates:
            extra = min(limit - given[i], max(1, remaining * portions[i] // pool), surplus)
            given[i] = given[i] + extra
            surplus = surplus - extra
    return np.array([limit] + given)


def ragged(own_key, amount, total, most, slope):
    if amount == 2:
        one = jax.random.randint(own_key, (), max(1, total - most), min(most, total - 1) + 1)
        return jnp.stack([one, total - one])
    tallies = jnp.asarray(profile(amount, total, most, slope), jnp.int32)
    couples = (amount - 1) // 2
    source_of, receiver = tallies[1:1 + 2 * couples:2], tallies[2:2 + 2 * couples:2]
    margin = jnp.minimum(source_of - 1, most - receiver)
    passed = jax.random.randint(jax.random.fold_in(own_key, 1), (couples,), 0, 1 << 20) % (margin + 1)
    tallies = tallies.at[1:1 + 2 * couples:2].set(source_of - passed).at[2:2 + 2 * couples:2].set(receiver + passed)
    return tallies[jax.random.permutation(jax.random.fold_in(own_key, 2), amount)]


def centred(key, shape, width, most, cuts=(), kind=jnp.bfloat16):
    array = width * jax.random.normal(key, shape, jnp.float32)
    if cuts:
        array = array * steps_of(key, shape, cuts, -0.22, 0.18)
    return jnp.clip(array, -most, most).astype(kind)


def setup_inputs(seed: int = 0) -> dict:
    key_list = jax.random.split(jax.random.key(seed), 5)
    return {
        "queries": draw_queries(jax.random.fold_in(key_list[4], 71), 0),
        "keys": draw_keys(jax.random.fold_in(key_list[4], 71), 0),
        "values": centred(key_list[2], (TOKENS, KVH, HD), 1.0, 6.0, ((0, 32),)),
        "doc_blocks": ragged(key_list[3], NDOCS, TOKENS // BLOCK, MAXBLK, 2).astype(jnp.int32),
    }


def segment_of(positions, doc_ends):
    return lax.optimization_barrier(jnp.sum((doc_ends[None, :] <= positions[:, None]).astype(jnp.int32), axis=1))

def reference(queries, keys, values, doc_blocks):
    group = QH // KVH
    reach = LOOK * TOK_DEV
    span = reach + TOK_DEV
    scale = 1.0 / math.sqrt(HD)
    doc_ends = jnp.cumsum(doc_blocks, dtype=jnp.int32) * BLOCK
    positions = jnp.arange(TOKENS, dtype=jnp.int32)
    documents = segment_of(positions, doc_ends)
    padded_keys = jnp.concatenate([jnp.zeros((reach, KVH, HD), keys.dtype), keys], axis=0)
    padded_values = jnp.concatenate([jnp.zeros((reach, KVH, HD), values.dtype), values], axis=0)
    padded_docs = jnp.concatenate([jnp.full((reach,), -1, jnp.int32), documents], axis=0)

    def one_shard(index):
        start = (index * TOK_DEV).astype(jnp.int32)
        query_block = lax.dynamic_slice_in_dim(queries, start, TOK_DEV, 0).reshape(TOK_DEV, KVH, group, HD).astype(jnp.float32)
        key_block = lax.dynamic_slice_in_dim(padded_keys, start, span, 0).astype(jnp.float32)
        value_block = lax.dynamic_slice_in_dim(padded_values, start, span, 0).astype(jnp.float32)
        key_docs = lax.dynamic_slice_in_dim(padded_docs, start, span, 0)
        query_docs = lax.dynamic_slice_in_dim(documents, start, TOK_DEV, 0)
        key_pos = start - reach + jnp.arange(span, dtype=jnp.int32)
        query_pos = start + jnp.arange(TOK_DEV, dtype=jnp.int32)
        allowed = (key_docs[None, :] == query_docs[:, None]) & (key_pos[None, :] <= query_pos[:, None])
        scores = jnp.einsum('tkgd,skd->kgts', query_block, key_block) * scale
        scores = jnp.where(allowed[None, None], scores, jnp.float32(-1e+30))
        top = lax.optimization_barrier(jnp.max(scores, axis=-1))
        weights = jnp.where(allowed[None, None], jnp.exp(scores - top[..., None]), jnp.float32(0.0))
        total = lax.optimization_barrier(jnp.sum(weights, axis=-1))
        rounded = lax.optimization_barrier(weights.astype(jnp.bfloat16)).astype(jnp.float32)
        summed = jnp.einsum('kgts,skd->kgtd', rounded, value_block)
        output = (summed / total[..., None]).transpose(2, 0, 1, 3).reshape(TOK_DEV, QH, HD)
        return output.astype(jnp.bfloat16)
    shards = lax.map(one_shard, jnp.arange(N_CTX, dtype=jnp.int32))
    return shards.reshape(TOKENS, QH, HD)
```

```python
import functools
import math

import jax
import jax.numpy as jnp
from jax import lax
from jax.experimental import pallas as pl
from jax.experimental.pallas import tpu as pltpu
from jax.sharding import PartitionSpec as P

BLOCK = 128
CHUNK = 16
UNROLL = 4
lowest = -1e30


def passed_along(shard, axis, by):
    size = lax.axis_size(axis)
    pairs = [(i, i + by) for i in range(size) if 0 <= i + by < size]
    return lax.ppermute(shard, axis, pairs)


def attend_kernel(scale, docs_ref, index_ref, query_ref, *refs):
    *shard_refs, out_ref, key_win, value_win = refs
    rows, heads, depth = query_ref.shape
    count = shard_refs[0].shape[2]
    group = heads // count
    reach = sum(ref.shape[0] * ref.shape[3] for ref in shard_refs[1:]) // BLOCK
    at = 0
    for ref in reversed(shard_refs):
        pieces, _, _, tokens, _ = ref.shape
        for piece in range(pieces):
            for head in range(count):
                lanes = slice(head * depth, (head + 1) * depth)
                key_win[at : at + tokens, lanes] = ref[piece, 0, head]
                value_win[at : at + tokens, lanes] = ref[piece, 1, head]
            at += tokens

    chunk_rows = CHUNK * heads
    row = lax.broadcasted_iota(jnp.int32, (chunk_rows, 1), 0)
    head_of = row % heads // group
    token_of = row // heads
    column = lax.broadcasted_iota(jnp.int32, (chunk_rows, BLOCK), 1)
    rate = scale * math.log2(math.e)

    def one_chunk(number, block, step):
        first = block * BLOCK + step * CHUNK
        query = query_ref[pl.ds(first, CHUNK)].reshape(chunk_rows, depth)
        spread = jnp.concatenate(
            [jnp.where(head_of == head, query, jnp.zeros_like(query)) for head in range(count)], axis=1
        )
        width = (number + 1) * BLOCK
        start = pl.multiple_of((reach + block - number) * BLOCK, BLOCK)
        scores = lax.dot_general(
            spread,
            key_win[pl.ds(start, width)],
            (((1,), (1,)), ((), ())),
            preferred_element_type=jnp.float32,
        )
        last = jnp.where(column <= token_of + step * CHUNK, scores[:, width - BLOCK :], lowest)
        if number:
            scores = jnp.concatenate([scores[:, : width - BLOCK], last], axis=1)
        else:
            scores = last
        top = jnp.max(scores, axis=1, keepdims=True)
        weights = jnp.exp2((scores - top) * rate)
        total = jnp.sum(weights, axis=1, keepdims=True)
        summed = jnp.dot(
            weights.astype(jnp.bfloat16), value_win[pl.ds(start, width)], preferred_element_type=jnp.float32
        )
        mine = summed[:, :depth]
        for head in range(1, count):
            mine = jnp.where(head_of == head, summed[:, head * depth : (head + 1) * depth], mine)
        out = (mine / total).astype(out_ref.dtype)
        out_ref[pl.ds(first, CHUNK)] = out.reshape(CHUNK, heads, depth)

    @pl.loop(0, rows // BLOCK)
    def _(block):
        own = index_ref[0] * (rows // BLOCK) + block
        start, behind = 0, 0
        for i in range(docs_ref.shape[0]):
            behind = jnp.where(own >= start, own - start, behind)
            start = start + docs_ref[i]
        for number in range(reach + 1):

            @pl.when(behind == number)
            def _():
                def body(step, carry):
                    one_chunk(number, block, step)
                    return carry

                lax.fori_loop(0, BLOCK // CHUNK, body, 0, unroll=UNROLL)


def body(queries, keys, values, doc_blocks):
    tokens, kv_heads, depth = keys.shape
    parts = lax.axis_size("kvh")
    count = kv_heads // parts
    rows, heads, _ = queries.shape
    sections = min(3, lax.axis_size("ctx") // 4)
    behind = 2**sections - 1
    both = jnp.stack([keys, values]).reshape(2, tokens, parts, count, depth).transpose(2, 0, 3, 1, 4)
    own = lax.all_to_all(both, "kvh", split_axis=0, concat_axis=0, tiled=True)
    shards = [own]
    for distance in range(1, behind + 1):
        sent = own if distance < behind else own[parts // 2 :]
        shards.append(passed_along(sent, "ctx", distance))
    index = lax.axis_index("ctx").astype(jnp.int32).reshape(1)
    reach = 2 * behind - 1
    window = (reach + 2) * BLOCK
    return pl.pallas_call(
        functools.partial(attend_kernel, 1.0 / math.sqrt(depth)),
        out_shape=jax.ShapeDtypeStruct(queries.shape, queries.dtype),
        in_specs=[pl.BlockSpec(memory_space=pltpu.SMEM)] * 2
        + [pl.BlockSpec(memory_space=pltpu.VMEM)] * (1 + len(shards)),
        out_specs=pl.BlockSpec(memory_space=pltpu.VMEM),
        scratch_shapes=[pltpu.VMEM((window, count * depth), jnp.bfloat16)] * 2,
        compiler_params=pltpu.CompilerParams(vmem_limit_bytes=32 * 1024 * 1024),
        name="attend",
    )(doc_blocks, index, queries, *shards)


def solution(mesh):
    in_specs = (
        P("ctx", "kvh", None),
        P(("ctx", "kvh"), None, None),
        P(("ctx", "kvh"), None, None),
        P(),
    )
    out_specs = P("ctx", "kvh", None)
    return jax.shard_map(body, mesh=mesh, in_specs=in_specs, out_specs=out_specs, check_vma=False)
```

```python
import functools
import math

import jax
import jax.numpy as jnp
from jax import lax
from jax.experimental import pallas as pl
from jax.experimental.pallas import tpu as pltpu
from jax.sharding import PartitionSpec as P

BLOCK = 128
CHUNK = 16
lowest = -1e30


def passed_along(shard, axis, by):
    size = lax.axis_size(axis)
    pairs = [(i, i + by) for i in range(size) if 0 <= i + by < size]
    return lax.ppermute(shard, axis, pairs)


def split_kernel(docs_ref, index_ref, key_ref, value_ref, out_ref, spans_ref, behind_ref, wide_keys, wide_values):
    parts, _, count, tokens, depth = out_ref.shape
    heads = parts * count
    for which, (ref, wide) in enumerate(((key_ref, wide_keys), (value_ref, wide_values))):
        wide[...] = ref[...].reshape(tokens * heads, depth).astype(jnp.float32)
        for head in range(heads):
            part = wide[pl.ds(head, tokens, stride=heads), :]
            out_ref[head // count, which, head % count] = part.astype(out_ref.dtype)
    blocks = behind_ref.shape[0]
    first = index_ref[0] * blocks
    spans, start = jnp.int32(0), jnp.int32(0)
    behind = [jnp.int32(0)] * blocks
    for i in range(docs_ref.shape[0]):
        for block in range(blocks):
            behind[block] = jnp.where(first + block >= start, first + block - start, behind[block])
        end = start + docs_ref[i]
        spans = jnp.maximum(spans, lax.div(end - 1, blocks) - lax.div(start, blocks))
        start = end
    spans_ref[0] = spans
    for block in range(blocks):
        behind_ref[block] = jnp.full(behind_ref.shape[1:], behind[block], jnp.int32)


def fill(shard_refs, key_win, value_win):
    at = 0
    for ref in reversed(shard_refs):
        pieces, _, count, tokens, depth = ref.shape
        group = BLOCK // tokens
        for piece in range(0, pieces, group):
            for head in range(count):
                lanes = slice(head * depth, (head + 1) * depth)
                key, value = (
                    jnp.concatenate([ref[piece + i, which, head] for i in range(group)], axis=0) for which in range(2)
                )
                key_win[lanes, at : at + BLOCK] = key.T
                value_win[at : at + BLOCK, lanes] = value
            at += BLOCK


def key_scores(count, heads, query, keys):
    head_of = lax.broadcasted_iota(jnp.int32, query.shape, 0) % heads // (heads // count)
    spread = jnp.concatenate(
        [jnp.where(head_of == head, query, jnp.zeros_like(query)) for head in range(count)], axis=1
    )
    return jnp.dot(spread, keys, preferred_element_type=jnp.float32)


def value_sums(count, heads, weights, values):
    wide = jnp.dot(weights.astype(jnp.bfloat16), values, preferred_element_type=jnp.float32)
    depth = wide.shape[1] // count
    tall = wide.reshape(wide.shape[0] // heads, count, heads // count, wide.shape[1])
    return jnp.concatenate(
        [tall[:, head : head + 1, :, head * depth : (head + 1) * depth] for head in range(count)], axis=1
    ).reshape(wide.shape[0], depth)


def lane_sums(weights):
    return sum(weights[:, at : at + BLOCK] for at in range(0, weights.shape[1], BLOCK))


def in_chunks(blocks, unrolled, work):
    steps = BLOCK // CHUNK
    if unrolled:
        for step in range(steps):
            for block in range(blocks):
                work(block, step)
    else:

        def every(step, carry):
            for block in range(blocks):
                work(block, step)
            return carry

        lax.fori_loop(0, steps, every, 0)


def own_kernel(scale, behind_ref, query_ref, shard_ref, summed_ref, top_ref, total_ref, key_win, value_win):
    rows, heads, depth = query_ref.shape
    count = shard_ref.shape[2]
    blocks = rows // BLOCK
    behind = [jnp.max(behind_ref[block]) for block in range(blocks)]
    fill([shard_ref], key_win, value_win)
    chunk_rows = CHUNK * heads
    ahead = lax.broadcasted_iota(jnp.int32, (chunk_rows, BLOCK), 1)
    ahead = ahead - lax.broadcasted_iota(jnp.int32, (chunk_rows, BLOCK), 0) // heads

    def work(numbers, block, step):
        start, width = (block - numbers[block]) * BLOCK, (numbers[block] + 1) * BLOCK
        first = block * BLOCK + step * CHUNK
        query = query_ref[pl.ds(first, CHUNK)].reshape(chunk_rows, depth)
        scores = key_scores(count, heads, query, key_win[:, start : start + width])
        last = jnp.where(ahead <= step * CHUNK, scores[:, width - BLOCK :], lowest)
        scores = jnp.concatenate([scores[:, : width - BLOCK], last], axis=1) if width > BLOCK else last
        top = jnp.max(scores, axis=1, keepdims=True)
        weights = jnp.exp2((scores - top) * (scale * math.log2(math.e)))
        at = pl.ds(first * heads, chunk_rows)
        top_ref[at] = jnp.broadcast_to(top, (chunk_rows, BLOCK))
        total_ref[at] = lane_sums(weights)
        summed_ref[at] = value_sums(count, heads, weights, value_win[start : start + width])

    joint = behind[1] >= 1 if blocks == 2 else None
    for same in (True, False):

        @pl.when(joint if same else jnp.logical_not(joint))
        def _():
            numbers = (0, int(same))
            in_chunks(blocks, True, functools.partial(work, numbers))


def join_kernel(scale, offset, final, behind_ref, query_ref, summed_in, top_in, total_in, *refs):
    outs = 1 if final else 3
    if final:
        *shard_refs, out_to, key_win, value_win, out_ref, left = refs
    else:
        shard_refs, (*out_refs, key_win, value_win) = refs[: -outs - 2], refs[-outs - 2 :]
    rows, heads, depth = query_ref.shape
    count = shard_refs[0].shape[2]
    blocks = rows // BLOCK
    window = value_win.shape[0] // BLOCK
    behind = [jnp.max(behind_ref[block]) for block in range(blocks)]
    fars = [jnp.clip(behind[block] - offset - block, 0, window) for block in range(blocks)]
    fill(shard_refs, key_win, value_win)
    chunk_rows = CHUNK * heads
    rate = scale * math.log2(math.e)

    def work(numbers, block, step):
        number = numbers[block]
        first = block * BLOCK + step * CHUNK
        at = pl.ds(first * heads, chunk_rows)
        if number:
            start, width = (window - number) * BLOCK, number * BLOCK
            query = query_ref[pl.ds(first, CHUNK)].reshape(chunk_rows, depth)
            scores = key_scores(count, heads, query, key_win[:, start : start + width])
            top_old = top_in[at]
            top = jnp.maximum(top_old, jnp.max(scores, axis=1, keepdims=True))
            fading = jnp.exp2((top_old - top) * rate)
            weights = jnp.exp2((scores - jnp.concatenate([top] * number, axis=1)) * rate)
            total = total_in[at] * fading + lane_sums(weights)
            summed = summed_in[at] * fading + value_sums(count, heads, weights, value_win[start : start + width])
        elif final:
            summed, total = summed_in[at], total_in[at]
        else:
            summed, top, total = summed_in[at], top_in[at], total_in[at]
        if final:
            whole = jnp.broadcast_to(jnp.sum(total, axis=1, keepdims=True), summed.shape)
            inverse = pl.reciprocal(whole, approx=True)
            inverse = inverse * (2.0 - whole * inverse)
            out = (summed * inverse).astype(out_ref.dtype)
            out_ref[pl.ds(first, CHUNK)] = out.reshape(CHUNK, heads, depth)
            at = pl.ds(first, CHUNK)
            pltpu.make_async_copy(out_ref.at[at], out_to.at[at], left).start()
        else:
            for ref, value in zip(out_refs, (summed, top, total)):
                ref[at] = value

    cases = [(0, 0)] + [(n, m) for n in range(1, window + 1) for m in sorted({0, min(n, window - (window % 2))})]
    for numbers in cases:

        @pl.when(jnp.logical_and(fars[0] == numbers[0], fars[1] == numbers[1]))
        def _():
            in_chunks(blocks, window <= 3, functools.partial(work, numbers))

    if final:
        pltpu.make_async_copy(out_ref, out_to, left).wait()


def body(queries, keys, values, doc_blocks):
    tokens, kv_heads, depth = keys.shape
    parts = lax.axis_size("kvh")
    count = kv_heads // parts
    rows, heads, _ = queries.shape
    sections = min(3, lax.axis_size("ctx") // 4)
    behind = 2**sections - 1
    per_shard = rows // BLOCK
    smem, vmem = pl.BlockSpec(memory_space=pltpu.SMEM), pl.BlockSpec(memory_space=pltpu.VMEM)
    params = pltpu.CompilerParams(vmem_limit_bytes=24 * 1024 * 1024)
    scale = 1.0 / math.sqrt(depth)
    light, heavy = (
        pl.CostEstimate(flops=flops, bytes_accessed=2**20, transcendentals=10**6) for flops in (10**8, 4 * 10**10)
    )
    shape = jax.ShapeDtypeStruct
    index = lax.axis_index("ctx").astype(jnp.int32).reshape(1)
    both, spans, nearer = pl.pallas_call(
        split_kernel,
        out_shape=(
            shape((parts, 2, count, tokens, depth), keys.dtype),
            shape((1,), jnp.int32),
            shape((per_shard, 8, 128), jnp.int32),
        ),
        in_specs=[smem] * 2 + [vmem] * 2,
        out_specs=(vmem, smem, vmem),
        scratch_shapes=[pltpu.VMEM((tokens * kv_heads, depth), jnp.float32)] * 2,
        name="split",
    )(doc_blocks, index, keys, values)
    own = lax.all_to_all(both, "kvh", split_axis=0, concat_axis=0, tiled=True)
    far = [passed_along(own, "ctx", 2)]
    one = passed_along(own, "ctx", 1)
    for distance in range(3, behind + 1):
        sent = own if distance < behind else own[parts // 2 :]
        send = functools.partial(passed_along, axis="ctx", by=distance)
        far.append(lax.cond(spans[0] >= distance, send, lambda x: x, sent))
    own, far[1:] = lax.optimization_barrier((own, far[1:]))

    state = [shape((rows * heads, depth), jnp.float32)] * 3

    def window(group):
        length = sum(s.shape[0] * s.shape[3] for s in group)
        return [
            pltpu.VMEM((count * depth, length), jnp.bfloat16),
            pltpu.VMEM((length, count * depth), jnp.bfloat16),
        ]

    kept = pl.pallas_call(
        functools.partial(own_kernel, scale),
        out_shape=state,
        in_specs=[vmem] * 3,
        out_specs=[vmem] * 3,
        scratch_shapes=window([own]),
        compiler_params=params,
        cost_estimate=light,
        name="own",
    )(nearer, queries, own)
    kept = pl.pallas_call(
        functools.partial(join_kernel, scale, 0, False),
        out_shape=state,
        in_specs=[vmem] * 6,
        out_specs=[vmem] * 3,
        scratch_shapes=window([one]),
        compiler_params=params,
        cost_estimate=heavy,
        name="one",
    )(nearer, queries, *kept, one)
    return pl.pallas_call(
        functools.partial(join_kernel, scale, per_shard, True),
        out_shape=shape(queries.shape, queries.dtype),
        in_specs=[vmem] * (5 + len(far)),
        out_specs=pl.BlockSpec(memory_space=pl.ANY),
        scratch_shapes=window(far) + [pltpu.VMEM(queries.shape, queries.dtype), pltpu.SemaphoreType.DMA],
        compiler_params=params,
        cost_estimate=light,
        name="far",
    )(nearer, queries, *kept, *far)


def solution(mesh):
    in_specs = (
        P("ctx", "kvh", None),
        P(("ctx", "kvh"), None, None),
        P(("ctx", "kvh"), None, None),
        P(),
    )
    out_specs = P("ctx", "kvh", None)
    return jax.shard_map(body, mesh=mesh, in_specs=in_specs, out_specs=out_specs, check_vma=False)
```

```python
import functools
import math

import jax
import jax.numpy as jnp
from jax import lax
from jax.experimental import pallas as pl
from jax.experimental.pallas import tpu as pltpu
from jax.sharding import PartitionSpec as P

BLOCK = 128
CHUNK = 16
TOGETHER = 8
lowest = -1e30


def passed_along(shard, axis, by):
    size = lax.axis_size(axis)
    pairs = [(i, i + by) for i in range(size) if 0 <= i + by < size]
    return lax.ppermute(shard, axis, pairs)


def plan_kernel(docs_ref, index_ref, spans_ref, behind_ref):
    blocks = behind_ref.shape[0]
    first = index_ref[0] * blocks
    spans, start = jnp.int32(0), jnp.int32(0)
    behind = [jnp.int32(0)] * blocks
    for i in range(docs_ref.shape[0]):
        for block in range(blocks):
            behind[block] = jnp.where(first + block >= start, first + block - start, behind[block])
        end = start + docs_ref[i]
        spans = jnp.maximum(spans, lax.div(end - 1, blocks) - lax.div(start, blocks))
        start = end
    spans_ref[0] = spans
    for block in range(blocks):
        behind_ref[block] = jnp.full(behind_ref.shape[1:], behind[block], jnp.int32)


def fill(shard_refs, key_win, value_win):
    at = 0
    for ref in reversed(shard_refs):
        pieces, count, tokens, depth = ref.shape
        depth = depth // 2
        group = BLOCK // tokens
        for piece in range(0, pieces, group):
            for head in range(count):
                lanes = slice(head * depth, (head + 1) * depth)
                key, value = (
                    jnp.concatenate([ref[piece + i, head, :, half] for i in range(group)], axis=0)
                    for half in (slice(0, depth), slice(depth, 2 * depth))
                )
                key_win[lanes, at : at + BLOCK] = key.T
                value_win[at : at + BLOCK, lanes] = value
            at += BLOCK


def key_scores(count, heads, query, keys):
    head_of = lax.broadcasted_iota(jnp.int32, query.shape, 0) % heads // (heads // count)
    spread = jnp.concatenate(
        [jnp.where(head_of == head, query, jnp.zeros_like(query)) for head in range(count)], axis=1
    )
    return jnp.dot(spread, keys, preferred_element_type=jnp.float32)


def value_sums(count, heads, weights, values):
    wide = jnp.dot(weights.astype(jnp.bfloat16), values, preferred_element_type=jnp.float32)
    depth = wide.shape[1] // count
    tall = wide.reshape(wide.shape[0] // heads, count, heads // count, wide.shape[1])
    return jnp.concatenate(
        [tall[:, head : head + 1, :, head * depth : (head + 1) * depth] for head in range(count)], axis=1
    ).reshape(wide.shape[0], depth)


def lane_sums(weights):
    return sum(weights[:, at : at + BLOCK] for at in range(0, weights.shape[1], BLOCK))


def in_chunks(blocks, work):
    steps = BLOCK // CHUNK

    def together(some, carry):
        for step in range(TOGETHER):
            for block in range(blocks):
                work(block, some * TOGETHER + step)
        return carry

    if TOGETHER == steps:
        together(0, None)
    else:
        lax.fori_loop(0, steps // TOGETHER, together, None)


def own_kernel(scale, behind_ref, query_ref, shard_ref, summed_ref, top_ref, total_ref, key_win, value_win):
    rows, heads, depth = query_ref.shape
    count = shard_ref.shape[1]
    blocks = rows // BLOCK
    behind = [jnp.max(behind_ref[block]) for block in range(blocks)]
    fill([shard_ref], key_win, value_win)
    chunk_rows = CHUNK * heads
    ahead = lax.broadcasted_iota(jnp.int32, (chunk_rows, BLOCK), 1)
    ahead = ahead - lax.broadcasted_iota(jnp.int32, (chunk_rows, BLOCK), 0) // heads

    def work(numbers, block, step):
        start, width = (block - numbers[block]) * BLOCK, (numbers[block] + 1) * BLOCK
        first = block * BLOCK + step * CHUNK
        query = query_ref[pl.ds(first, CHUNK)].reshape(chunk_rows, depth)
        scores = key_scores(count, heads, query, key_win[:, start : start + width])
        last = jnp.where(ahead <= step * CHUNK, scores[:, width - BLOCK :], lowest)
        scores = jnp.concatenate([scores[:, : width - BLOCK], last], axis=1) if width > BLOCK else last
        top = jnp.max(scores, axis=1, keepdims=True)
        weights = jnp.exp2((scores - top) * (scale * math.log2(math.e)))
        at = pl.ds(pl.multiple_of(first * heads, chunk_rows), chunk_rows)
        top_ref[at] = jnp.broadcast_to(top, (chunk_rows, BLOCK))
        total_ref[at] = lane_sums(weights)
        summed_ref[at] = value_sums(count, heads, weights, value_win[start : start + width])

    joint = behind[1] >= 1 if blocks == 2 else None
    for same in (True, False):

        @pl.when(joint if same else jnp.logical_not(joint))
        def _():
            numbers = (0, int(same))
            in_chunks(blocks, functools.partial(work, numbers))


def join_kernel(scale, offset, final, behind_ref, query_ref, summed_in, top_in, total_in, *refs):
    outs = 1 if final else 3
    if final:
        *shard_refs, out_to, key_win, value_win, out_ref, left = refs
    else:
        shard_refs, (*out_refs, key_win, value_win) = refs[: -outs - 2], refs[-outs - 2 :]
    rows, heads, depth = query_ref.shape
    count = shard_refs[0].shape[1]
    blocks = rows // BLOCK
    window = value_win.shape[0] // BLOCK
    behind = [jnp.max(behind_ref[block]) for block in range(blocks)]
    fars = [jnp.clip(behind[block] - offset - block, 0, window) for block in range(blocks)]
    fill(shard_refs, key_win, value_win)
    chunk_rows = CHUNK * heads
    rate = scale * math.log2(math.e)

    def work(taking, block, step):
        first = block * BLOCK + step * CHUNK
        at = pl.ds(pl.multiple_of(first * heads, chunk_rows), chunk_rows)
        if taking[block]:
            start = (window - taking[block]) * BLOCK
            query = query_ref[pl.ds(first, CHUNK)].reshape(chunk_rows, depth)
            scores = key_scores(count, heads, query, key_win[:, start:]) + hidden[block][:, start:]
            top_old = top_in[at]
            top = jnp.maximum(top_old, jnp.max(scores, axis=1, keepdims=True))
            fading = jnp.exp2((top_old - top) * rate)
            weights = jnp.exp2((scores - jnp.concatenate([top] * taking[block], axis=1)) * rate)
            total = total_in[at] * fading + lane_sums(weights)
            summed = summed_in[at] * fading + value_sums(count, heads, weights, value_win[start:])
        elif final:
            summed, total = summed_in[at], total_in[at]
        else:
            summed, top, total = summed_in[at], top_in[at], total_in[at]
        if final:
            out = (summed / jnp.sum(total, axis=1, keepdims=True)).astype(out_ref.dtype)
            out_ref[pl.ds(first, CHUNK)] = out.reshape(CHUNK, heads, depth)
            at = pl.ds(first, CHUNK)
            pltpu.make_async_copy(out_ref.at[at], out_to.at[at], left).start()
        else:
            for ref, value in zip(out_refs, (summed, top, total)):
                ref[at] = value

    column = lax.broadcasted_iota(jnp.int32, (1, window * BLOCK), 1)
    hidden = [jnp.where(column < (window - far) * BLOCK, lowest, 0.0) for far in fars]
    levels = sorted({0, min(2, window), window})
    even = window - window % 2
    cases = [(0, 0)] + [(n, m) for n in levels[1:] for m in sorted({0, 2, min(n, even)})]
    needed = [sum(jnp.where(far > low, high - low, 0) for low, high in zip(levels, levels[1:])) for far in fars]
    needed[1] = jnp.minimum(needed[1], even)
    for taking in cases:

        @pl.when(jnp.logical_and(needed[0] == taking[0], needed[1] == taking[1]))
        def _():
            in_chunks(blocks, functools.partial(work, taking))

    if final:
        pltpu.make_async_copy(out_ref, out_to, left).wait()


def body(queries, keys, values, doc_blocks):
    tokens, kv_heads, depth = keys.shape
    parts = lax.axis_size("kvh")
    count = kv_heads // parts
    rows, heads, _ = queries.shape
    sections = min(3, lax.axis_size("ctx") // 4)
    behind = 2**sections - 1
    per_shard = rows // BLOCK
    smem, vmem = pl.BlockSpec(memory_space=pltpu.SMEM), pl.BlockSpec(memory_space=pltpu.VMEM)
    params = pltpu.CompilerParams(vmem_limit_bytes=24 * 1024 * 1024)
    scale = 1.0 / math.sqrt(depth)
    light, heavy = (
        pl.CostEstimate(flops=flops, bytes_accessed=2**20, transcendentals=10**6) for flops in (10**8, 4 * 10**10)
    )
    shape = jax.ShapeDtypeStruct
    index = lax.axis_index("ctx").astype(jnp.int32).reshape(1)
    spans, nearer = pl.pallas_call(
        plan_kernel,
        out_shape=(shape((1,), jnp.int32), shape((per_shard, 8, 128), jnp.int32)),
        in_specs=[smem] * 2,
        out_specs=(smem, vmem),
        cost_estimate=light,
        name="plan",
    )(doc_blocks, index)
    both = lax.optimization_barrier(jnp.concatenate([keys, values], axis=2))
    both = both.reshape(tokens, parts, count, 2 * depth).transpose(1, 2, 0, 3)
    own = lax.all_to_all(both, "kvh", split_axis=0, concat_axis=0, tiled=True)
    far = [passed_along(own, "ctx", 2)]
    one = passed_along(own, "ctx", 1)
    for distance in range(3, behind + 1):
        sent = own if distance < behind else own[parts // 2 :]
        send = functools.partial(passed_along, axis="ctx", by=distance)
        far.append(lax.cond(spans[0] >= distance, send, lambda x: x, sent))
    own, far[1:] = lax.optimization_barrier((own, far[1:]))

    state = [shape((rows * heads, depth), jnp.float32)] * 3

    def window(group):
        length = sum(s.shape[0] * s.shape[2] for s in group)
        return [
            pltpu.VMEM((count * depth, length), jnp.bfloat16),
            pltpu.VMEM((length, count * depth), jnp.bfloat16),
        ]

    kept = pl.pallas_call(
        functools.partial(own_kernel, scale),
        out_shape=state,
        in_specs=[vmem] * 3,
        out_specs=[vmem] * 3,
        scratch_shapes=window([own]),
        compiler_params=params,
        cost_estimate=light,
        name="own",
    )(nearer, queries, own)
    kept = pl.pallas_call(
        functools.partial(join_kernel, scale, 0, False),
        out_shape=state,
        in_specs=[vmem] * 6,
        out_specs=[vmem] * 3,
        scratch_shapes=window([one]),
        compiler_params=params,
        cost_estimate=heavy,
        name="one",
    )(nearer, queries, *kept, one)
    return pl.pallas_call(
        functools.partial(join_kernel, scale, per_shard, True),
        out_shape=shape(queries.shape, queries.dtype),
        in_specs=[vmem] * (5 + len(far)),
        out_specs=pl.BlockSpec(memory_space=pl.ANY),
        scratch_shapes=window(far) + [pltpu.VMEM(queries.shape, queries.dtype), pltpu.SemaphoreType.DMA],
        compiler_params=params,
        cost_estimate=light,
        name="far",
    )(nearer, queries, *kept, *far)


def solution(mesh):
    in_specs = (
        P("ctx", "kvh", None),
        P(("ctx", "kvh"), None, None),
        P(("ctx", "kvh"), None, None),
        P(),
    )
    out_specs = P("ctx", "kvh", None)
    return jax.shard_map(body, mesh=mesh, in_specs=in_specs, out_specs=out_specs, check_vma=False)
```

```python
import functools
import math

import jax
import jax.numpy as jnp
from jax import lax
from jax.experimental import pallas as pl
from jax.experimental.pallas import tpu as pltpu
from jax.sharding import PartitionSpec as P

BLOCK = 128
CHUNK = 16
TOGETHER = 8
lowest = -1e30


def passed_along(shard, axis, by, parity=None):
    size = lax.axis_size(axis)
    pairs = [(i, (i + by) % size) for i in range(size)]
    if parity is not None:
        pairs = [(i, far if i % 2 == parity else i ^ 1) for i, far in pairs]
    return lax.ppermute(shard, axis, pairs)


def exchanged(pieces, axis):
    size = lax.axis_size(axis)
    me = lax.axis_index(axis)
    bits = size.bit_length() - 1
    shape = pieces.shape
    pieces = pieces.reshape(*[2] * bits, *shape[1:])
    for bit in range(bits):
        flipped = jnp.flip(pieces, bits - 1 - bit)
        pieces = jnp.where((me >> bit) & 1 == 1, flipped, pieces)
    pieces = pieces.reshape(shape)
    held = [pieces[0]]
    for other in range(1, size):
        held.append(lax.ppermute(pieces[other], axis, [(i, i ^ other) for i in range(size)]))
    return jnp.stack(held)


def plan_kernel(parts, longest, docs_ref, index_ref, spans_ref, last_ref, behind_ref):
    blocks = behind_ref.shape[0] - 1
    first = lax.div(index_ref[0], parts) * blocks
    spans, even, odd, start = jnp.int32(0), jnp.int32(0), jnp.int32(0), jnp.int32(0)
    behind = [jnp.int32(0)] * blocks
    for i in range(docs_ref.shape[0]):
        for block in range(blocks):
            behind[block] = jnp.where(first + block >= start, first + block - start, behind[block])
        end = start + docs_ref[i]
        head = lax.div(start, blocks)
        span = lax.div(end - 1, blocks) - head
        spans = jnp.maximum(spans, span)
        even = jnp.where((span >= longest) & (head % 2 == 0), 1, even)
        odd = jnp.where((span >= longest) & (head % 2 == 1), 2, odd)
        start = end
    spans_ref[0] = spans
    last_ref[0] = even + odd
    for row, number in enumerate((*behind, lax.rem(index_ref[0], parts))):
        behind_ref[row] = jnp.full(behind_ref.shape[1:], number, jnp.int32)


def fill(me, shard_refs, key_win, value_win):
    at = 0
    for ref in reversed(shard_refs):
        pieces, count, tokens, depth = ref.shape
        depth = depth // 2
        group = BLOCK // tokens
        for piece in range(0, pieces, group):
            for head in range(count):
                lanes = slice(head * depth, (head + 1) * depth)
                key, value = (
                    jnp.concatenate([ref[((piece + i) ^ me) % pieces, head, :, half] for i in range(group)], axis=0)
                    for half in (slice(0, depth), slice(depth, 2 * depth))
                )
                key_win[lanes, at : at + BLOCK] = key.T
                value_win[at : at + BLOCK, lanes] = value
            at += BLOCK


def key_scores(count, heads, query, keys):
    head_of = lax.broadcasted_iota(jnp.int32, query.shape, 0) % heads // (heads // count)
    spread = jnp.concatenate(
        [jnp.where(head_of == head, query, jnp.zeros_like(query)) for head in range(count)], axis=1
    )
    return jnp.dot(spread, keys, preferred_element_type=jnp.float32)


def value_sums(count, heads, weights, values):
    wide = jnp.dot(weights.astype(jnp.bfloat16), values, preferred_element_type=jnp.float32)
    depth = wide.shape[1] // count
    tall = wide.reshape(wide.shape[0] // heads, count, heads // count, wide.shape[1])
    return jnp.concatenate(
        [tall[:, head : head + 1, :, head * depth : (head + 1) * depth] for head in range(count)], axis=1
    ).reshape(wide.shape[0], depth)


def lane_sums(weights):
    return sum(weights[:, at : at + BLOCK] for at in range(0, weights.shape[1], BLOCK))


def in_chunks(blocks, work):
    steps = BLOCK // CHUNK

    def together(some, carry):
        for step in range(TOGETHER):
            for block in range(blocks):
                work(block, some * TOGETHER + step)
        return carry

    if TOGETHER == steps:
        together(0, None)
    else:
        lax.fori_loop(0, steps // TOGETHER, together, None)


def own_kernel(scale, behind_ref, query_ref, shard_ref, summed_ref, top_ref, total_ref, key_win, value_win):
    rows, heads, depth = query_ref.shape
    count = shard_ref.shape[1]
    blocks = rows // BLOCK
    *behind, me = [jnp.max(behind_ref[row]) for row in range(blocks + 1)]
    fill(me, [shard_ref], key_win, value_win)
    chunk_rows = CHUNK * heads
    ahead = lax.broadcasted_iota(jnp.int32, (chunk_rows, BLOCK), 1)
    ahead = ahead - lax.broadcasted_iota(jnp.int32, (chunk_rows, BLOCK), 0) // heads

    def work(numbers, block, step):
        start, width = (block - numbers[block]) * BLOCK, (numbers[block] + 1) * BLOCK
        first = block * BLOCK + step * CHUNK
        query = query_ref[pl.ds(first, CHUNK)].reshape(chunk_rows, depth)
        scores = key_scores(count, heads, query, key_win[:, start : start + width])
        last = jnp.where(ahead <= step * CHUNK, scores[:, width - BLOCK :], lowest)
        scores = jnp.concatenate([scores[:, : width - BLOCK], last], axis=1) if width > BLOCK else last
        top = jnp.max(scores, axis=1, keepdims=True)
        weights = jnp.exp2((scores - top) * (scale * math.log2(math.e)))
        at = pl.ds(pl.multiple_of(first * heads, chunk_rows), chunk_rows)
        top_ref[at] = jnp.broadcast_to(top, (chunk_rows, BLOCK))
        total_ref[at] = lane_sums(weights)
        summed_ref[at] = value_sums(count, heads, weights, value_win[start : start + width])

    joint = behind[1] >= 1 if blocks == 2 else None
    for same in (True, False):

        @pl.when(joint if same else jnp.logical_not(joint))
        def _():
            numbers = (0, int(same))
            in_chunks(blocks, functools.partial(work, numbers))


def join_kernel(scale, offset, final, behind_ref, query_ref, summed_in, top_in, total_in, *refs):
    outs = 1 if final else 3
    if final:
        *shard_refs, out_to, key_win, value_win, out_ref, left = refs
    else:
        shard_refs, (*out_refs, key_win, value_win) = refs[: -outs - 2], refs[-outs - 2 :]
    rows, heads, depth = query_ref.shape
    count = shard_refs[0].shape[1]
    blocks = rows // BLOCK
    window = value_win.shape[0] // BLOCK
    *behind, me = [jnp.max(behind_ref[row]) for row in range(blocks + 1)]
    fars = [jnp.clip(behind[block] - offset - block, 0, window) for block in range(blocks)]
    fill(me, shard_refs, key_win, value_win)
    chunk_rows = CHUNK * heads
    rate = scale * math.log2(math.e)

    def work(taking, block, step):
        first = block * BLOCK + step * CHUNK
        at = pl.ds(pl.multiple_of(first * heads, chunk_rows), chunk_rows)
        if taking[block]:
            start = (window - taking[block]) * BLOCK
            query = query_ref[pl.ds(first, CHUNK)].reshape(chunk_rows, depth)
            scores = key_scores(count, heads, query, key_win[:, start:]) + hidden[block][:, start:]
            top_old = top_in[at]
            top = jnp.maximum(top_old, jnp.max(scores, axis=1, keepdims=True))
            fading = jnp.exp2((top_old - top) * rate)
            weights = jnp.exp2((scores - jnp.concatenate([top] * taking[block], axis=1)) * rate)
            total = total_in[at] * fading + lane_sums(weights)
            summed = summed_in[at] * fading + value_sums(count, heads, weights, value_win[start:])
        elif final:
            summed, total = summed_in[at], total_in[at]
        else:
            summed, top, total = summed_in[at], top_in[at], total_in[at]
        if final:
            out = (summed / jnp.sum(total, axis=1, keepdims=True)).astype(out_ref.dtype)
            out_ref[pl.ds(first, CHUNK)] = out.reshape(CHUNK, heads, depth)
            at = pl.ds(first, CHUNK)
            pltpu.make_async_copy(out_ref.at[at], out_to.at[at], left).start()
        else:
            for ref, value in zip(out_refs, (summed, top, total)):
                ref[at] = value

    column = lax.broadcasted_iota(jnp.int32, (1, window * BLOCK), 1)
    hidden = [jnp.where(column < (window - far) * BLOCK, lowest, 0.0) for far in fars]
    levels = sorted({0, min(2, window), window})
    even = window - window % 2
    cases = [(0, 0)] + [(n, m) for n in levels[1:] for m in sorted({0, 2, min(n, even)})]
    needed = [sum(jnp.where(far > low, high - low, 0) for low, high in zip(levels, levels[1:])) for far in fars]
    needed[1] = jnp.minimum(needed[1], even)
    for taking in cases:

        @pl.when(jnp.logical_and(needed[0] == taking[0], needed[1] == taking[1]))
        def _():
            in_chunks(blocks, functools.partial(work, taking))

    if final:
        pltpu.make_async_copy(out_ref, out_to, left).wait()


def body(queries, keys, values, doc_blocks):
    tokens, kv_heads, depth = keys.shape
    parts = lax.axis_size("kvh")
    count = kv_heads // parts
    rows, heads, _ = queries.shape
    sections = min(3, lax.axis_size("ctx") // 4)
    behind = 2**sections - 1
    per_shard = rows // BLOCK
    smem, vmem = pl.BlockSpec(memory_space=pltpu.SMEM), pl.BlockSpec(memory_space=pltpu.VMEM)
    params = pltpu.CompilerParams(vmem_limit_bytes=24 * 1024 * 1024)
    scale = 1.0 / math.sqrt(depth)
    light, heavy = (
        pl.CostEstimate(flops=flops, bytes_accessed=2**20, transcendentals=10**6) for flops in (10**8, 4 * 10**10)
    )
    shape = jax.ShapeDtypeStruct
    me = lax.axis_index("kvh")
    index = (lax.axis_index("ctx") * parts + me).astype(jnp.int32).reshape(1)
    spans, last, nearer = pl.pallas_call(
        functools.partial(plan_kernel, parts, behind),
        out_shape=(shape((1,), jnp.int32), shape((1,), jnp.int32), shape((per_shard + 1, 8, 128), jnp.int32)),
        in_specs=[smem] * 2,
        out_specs=(smem, smem, vmem),
        cost_estimate=light,
        name="plan",
    )(doc_blocks, index)
    both = lax.optimization_barrier(jnp.concatenate([keys, values], axis=2))
    both = both.reshape(tokens, parts, count, 2 * depth).transpose(1, 2, 0, 3)
    own = exchanged(both, "kvh")
    far = [passed_along(own, "ctx", 2)]
    one = passed_along(own, "ctx", 1)
    for distance in range(3, behind):
        send = functools.partial(passed_along, axis="ctx", by=distance)
        far.append(lax.cond(spans[0] >= distance, send, lambda x: x, own))
    half = parts // 2
    sent = jnp.where(me >= half, own[:half], own[half:])
    sends = [functools.partial(passed_along, axis="ctx", by=behind, parity=parity) for parity in (0, 1, None)]
    far.append(lax.switch(last[0], [lambda x: x, *sends], sent))
    own, far[1:] = lax.optimization_barrier((own, far[1:]))

    state = [shape((rows * heads, depth), jnp.float32)] * 3

    def window(group):
        length = sum(s.shape[0] * s.shape[2] for s in group)
        return [
            pltpu.VMEM((count * depth, length), jnp.bfloat16),
            pltpu.VMEM((length, count * depth), jnp.bfloat16),
        ]

    kept = pl.pallas_call(
        functools.partial(own_kernel, scale),
        out_shape=state,
        in_specs=[vmem] * 3,
        out_specs=[vmem] * 3,
        scratch_shapes=window([own]),
        compiler_params=params,
        cost_estimate=light,
        name="own",
    )(nearer, queries, own)
    kept = pl.pallas_call(
        functools.partial(join_kernel, scale, 0, False),
        out_shape=state,
        in_specs=[vmem] * 6,
        out_specs=[vmem] * 3,
        scratch_shapes=window([one]),
        compiler_params=params,
        cost_estimate=heavy,
        name="one",
    )(nearer, queries, *kept, one)
    return pl.pallas_call(
        functools.partial(join_kernel, scale, per_shard, True),
        out_shape=shape(queries.shape, queries.dtype),
        in_specs=[vmem] * (5 + len(far)),
        out_specs=pl.BlockSpec(memory_space=pl.ANY),
        scratch_shapes=window(far) + [pltpu.VMEM(queries.shape, queries.dtype), pltpu.SemaphoreType.DMA],
        compiler_params=params,
        cost_estimate=light,
        name="far",
    )(nearer, queries, *kept, *far)


def solution(mesh):
    in_specs = (
        P("ctx", "kvh", None),
        P(("ctx", "kvh"), None, None),
        P(("ctx", "kvh"), None, None),
        P(),
    )
    out_specs = P("ctx", "kvh", None)
    return jax.shard_map(body, mesh=mesh, in_specs=in_specs, out_specs=out_specs, check_vma=False)
```

```python
import functools
import math

import jax
import jax.numpy as jnp
from jax import lax
from jax.experimental import pallas as pl
from jax.experimental.pallas import tpu as pltpu
from jax.sharding import PartitionSpec as P

BLOCK = 128
CHUNK = 16
TOGETHER = 8
lowest = -1e30


def passed_along(piece, by, across=0, parity=None):
    shards, parts = lax.axis_size("ctx"), lax.axis_size("kvh")
    pairs = []
    for shard in range(shards):
        to = (shard + by) % shards if parity is None or shard % 2 == parity else shard ^ 1
        pairs += [(shard * parts + part, to * parts + (part ^ across)) for part in range(parts)]
    return lax.ppermute(piece, ("ctx", "kvh"), pairs)


def for_groups(pieces, me):
    pieces = pieces.reshape(2, 2, *pieces.shape[1:])
    pieces = jnp.where(me & 1 == 1, jnp.flip(pieces, 1), pieces)
    return jnp.where(me >> 1 == 1, jnp.flip(pieces, 0), pieces)


def plan_kernel(parts, longest, docs_ref, index_ref, spans_ref, last_ref, behind_ref):
    blocks = behind_ref.shape[0] - 1
    first = lax.div(index_ref[0], parts) * blocks
    spans, even, odd, start = jnp.int32(0), jnp.int32(0), jnp.int32(0), jnp.int32(0)
    behind = [jnp.int32(0)] * blocks
    for i in range(docs_ref.shape[0]):
        for block in range(blocks):
            behind[block] = jnp.where(first + block >= start, first + block - start, behind[block])
        end = start + docs_ref[i]
        head = lax.div(start, blocks)
        span = lax.div(end - 1, blocks) - head
        spans = jnp.maximum(spans, span)
        even = jnp.where((span >= longest) & (head % 2 == 0), 1, even)
        odd = jnp.where((span >= longest) & (head % 2 == 1), 2, odd)
        start = end
    spans_ref[0] = spans
    last_ref[0] = even + odd
    for row, number in enumerate((*behind, lax.rem(index_ref[0], parts))):
        behind_ref[row] = jnp.full(behind_ref.shape[1:], number, jnp.int32)


def fill(me, shard_refs, key_win, value_win):
    core, side = me & 1, me >> 1
    at = 0
    for refs in reversed(shard_refs):
        for apart, ref in enumerate(refs):
            _, count, _, depth = ref.shape
            depth = depth // 2
            block = (side ^ apart) if len(refs) > 1 else 0
            rows = pl.ds(pl.multiple_of(at + block * BLOCK, BLOCK), BLOCK)
            for head in range(count):
                lanes = slice(head * depth, (head + 1) * depth)
                key, value = (
                    jnp.concatenate([ref[i ^ core, head, :, half] for i in range(2)], axis=0)
                    for half in (slice(0, depth), slice(depth, 2 * depth))
                )
                key_win[lanes, rows] = key.T
                value_win[rows, lanes] = value
        at += BLOCK * len(refs)


def key_scores(count, heads, query, keys):
    head_of = lax.broadcasted_iota(jnp.int32, query.shape, 0) % heads // (heads // count)
    spread = jnp.concatenate(
        [jnp.where(head_of == head, query, jnp.zeros_like(query)) for head in range(count)], axis=1
    )
    return jnp.dot(spread, keys, preferred_element_type=jnp.float32)


def value_sums(count, heads, weights, values):
    wide = jnp.dot(weights.astype(jnp.bfloat16), values, preferred_element_type=jnp.float32)
    depth = wide.shape[1] // count
    tall = wide.reshape(wide.shape[0] // heads, count, heads // count, wide.shape[1])
    return jnp.concatenate(
        [tall[:, head : head + 1, :, head * depth : (head + 1) * depth] for head in range(count)], axis=1
    ).reshape(wide.shape[0], depth)


def lane_sums(weights):
    return sum(weights[:, at : at + BLOCK] for at in range(0, weights.shape[1], BLOCK))


def in_chunks(blocks, work):
    steps = BLOCK // CHUNK

    def together(some, carry):
        for step in range(TOGETHER):
            for block in range(blocks):
                work(block, some * TOGETHER + step)
        return carry

    if TOGETHER == steps:
        together(0, None)
    else:
        lax.fori_loop(0, steps // TOGETHER, together, None)


def own_kernel(scale, behind_ref, query_ref, *refs):
    *shard_refs, summed_ref, top_ref, total_ref, key_win, value_win = refs
    rows, heads, depth = query_ref.shape
    count = shard_refs[0].shape[1]
    blocks = rows // BLOCK
    *behind, me = [jnp.max(behind_ref[row]) for row in range(blocks + 1)]
    fill(me, [shard_refs], key_win, value_win)
    chunk_rows = CHUNK * heads
    ahead = lax.broadcasted_iota(jnp.int32, (chunk_rows, BLOCK), 1)
    ahead = ahead - lax.broadcasted_iota(jnp.int32, (chunk_rows, BLOCK), 0) // heads

    def work(numbers, block, step):
        start, width = (block - numbers[block]) * BLOCK, (numbers[block] + 1) * BLOCK
        first = block * BLOCK + step * CHUNK
        query = query_ref[pl.ds(first, CHUNK)].reshape(chunk_rows, depth)
        scores = key_scores(count, heads, query, key_win[:, start : start + width])
        last = jnp.where(ahead <= step * CHUNK, scores[:, width - BLOCK :], lowest)
        scores = jnp.concatenate([scores[:, : width - BLOCK], last], axis=1) if width > BLOCK else last
        top = jnp.max(scores, axis=1, keepdims=True)
        weights = jnp.exp2((scores - top) * (scale * math.log2(math.e)))
        at = pl.ds(pl.multiple_of(first * heads, chunk_rows), chunk_rows)
        top_ref[at] = jnp.broadcast_to(top, (chunk_rows, BLOCK))
        total_ref[at] = lane_sums(weights)
        summed_ref[at] = value_sums(count, heads, weights, value_win[start : start + width])

    joint = behind[1] >= 1 if blocks == 2 else None
    for same in (True, False):

        @pl.when(joint if same else jnp.logical_not(joint))
        def _():
            numbers = (0, int(same))
            in_chunks(blocks, functools.partial(work, numbers))


def join_kernel(scale, offset, final, behind_ref, query_ref, summed_in, top_in, total_in, *refs):
    outs = 1 if final else 3
    if final:
        *shard_refs, out_to, key_win, value_win, out_ref, left = refs
    else:
        shard_refs, (*out_refs, key_win, value_win) = refs[: -outs - 2], refs[-outs - 2 :]
    rows, heads, depth = query_ref.shape
    count = shard_refs[0].shape[1]
    groups = [shard_refs[i : i + 2] for i in range(0, len(shard_refs), 2)]
    blocks = rows // BLOCK
    window = value_win.shape[0] // BLOCK
    *behind, me = [jnp.max(behind_ref[row]) for row in range(blocks + 1)]
    fars = [jnp.clip(behind[block] - offset - block, 0, window) for block in range(blocks)]
    fill(me, groups, key_win, value_win)
    chunk_rows = CHUNK * heads
    rate = scale * math.log2(math.e)

    def work(taking, block, step):
        first = block * BLOCK + step * CHUNK
        at = pl.ds(pl.multiple_of(first * heads, chunk_rows), chunk_rows)
        if taking[block]:
            start = (window - taking[block]) * BLOCK
            query = query_ref[pl.ds(first, CHUNK)].reshape(chunk_rows, depth)
            scores = key_scores(count, heads, query, key_win[:, start:]) + hidden[block][:, start:]
            top_old = top_in[at]
            top = jnp.maximum(top_old, jnp.max(scores, axis=1, keepdims=True))
            fading = jnp.exp2((top_old - top) * rate)
            weights = jnp.exp2((scores - jnp.concatenate([top] * taking[block], axis=1)) * rate)
            total = total_in[at] * fading + lane_sums(weights)
            summed = summed_in[at] * fading + value_sums(count, heads, weights, value_win[start:])
        elif final:
            summed, total = summed_in[at], total_in[at]
        else:
            summed, top, total = summed_in[at], top_in[at], total_in[at]
        if final:
            out = (summed / jnp.sum(total, axis=1, keepdims=True)).astype(out_ref.dtype)
            out_ref[pl.ds(first, CHUNK)] = out.reshape(CHUNK, heads, depth)
            at = pl.ds(first, CHUNK)
            pltpu.make_async_copy(out_ref.at[at], out_to.at[at], left).start()
        else:
            for ref, value in zip(out_refs, (summed, top, total)):
                ref[at] = value

    column = lax.broadcasted_iota(jnp.int32, (1, window * BLOCK), 1)
    hidden = [jnp.where(column < (window - far) * BLOCK, lowest, 0.0) for far in fars]
    levels = sorted({0, min(2, window), window})
    even = window - window % 2
    cases = [(0, 0)] + [(n, m) for n in levels[1:] for m in sorted({0, 2, min(n, even)})]
    needed = [sum(jnp.where(far > low, high - low, 0) for low, high in zip(levels, levels[1:])) for far in fars]
    needed[1] = jnp.minimum(needed[1], even)
    for taking in cases:

        @pl.when(jnp.logical_and(needed[0] == taking[0], needed[1] == taking[1]))
        def _():
            in_chunks(blocks, functools.partial(work, taking))

    if final:
        pltpu.make_async_copy(out_ref, out_to, left).wait()


def body(queries, keys, values, doc_blocks):
    tokens, kv_heads, depth = keys.shape
    parts = lax.axis_size("kvh")
    count = kv_heads // parts
    rows, heads, _ = queries.shape
    sections = min(3, lax.axis_size("ctx") // 4)
    behind = 2**sections - 1
    per_shard = rows // BLOCK
    smem, vmem = pl.BlockSpec(memory_space=pltpu.SMEM), pl.BlockSpec(memory_space=pltpu.VMEM)
    params = pltpu.CompilerParams(vmem_limit_bytes=24 * 1024 * 1024)
    scale = 1.0 / math.sqrt(depth)
    light, medium = (
        pl.CostEstimate(flops=flops, bytes_accessed=2**20, transcendentals=10**6) for flops in (10**8, 10**9)
    )
    shape = jax.ShapeDtypeStruct
    me = lax.axis_index("kvh")
    index = (lax.axis_index("ctx") * parts + me).astype(jnp.int32).reshape(1)
    spans, last, nearer = pl.pallas_call(
        functools.partial(plan_kernel, parts, behind),
        cost_estimate=medium,
        out_shape=(shape((1,), jnp.int32), shape((1,), jnp.int32), shape((per_shard + 1, 8, 128), jnp.int32)),
        in_specs=[smem] * 2,
        out_specs=(smem, smem, vmem),
        name="plan",
    )(doc_blocks, index)
    both = lax.optimization_barrier(jnp.concatenate([keys, values], axis=2))
    both = both.reshape(tokens, parts, count, 2 * depth).transpose(1, 2, 0, 3)
    pieces = for_groups(both, me)
    swapped = passed_along(pieces[:, 1], 0, across=1)
    here, there = (jnp.stack([pieces[side, 0], swapped[side]]) for side in range(2))
    own = [here, passed_along(there, 0, across=2)]
    far = [passed_along(here, 2), passed_along(there, 2, across=2)]
    one = [passed_along(here, 1), passed_along(there, 1, across=2)]
    for distance in range(3, behind):
        send = functools.partial(passed_along, by=distance)
        far += [lax.cond(spans[0] >= distance, send, lambda x: x, x) for x in own]

    def late(parity):
        return lambda *halves: passed_along(jnp.where(me >= parts // 2, *halves), behind, parity=parity)

    far.append(lax.switch(last[0], [lambda *halves: halves[0], late(0), late(1), late(None)], *own))
    own, far[2:] = lax.optimization_barrier((own, far[2:]))

    state = [shape((rows * heads, depth), jnp.float32)] * 3

    def window(group):
        length = sum(s.shape[0] * s.shape[2] for s in group)
        return [
            pltpu.VMEM((count * depth, length), jnp.bfloat16),
            pltpu.VMEM((length, count * depth), jnp.bfloat16),
        ]

    kept = pl.pallas_call(
        functools.partial(own_kernel, scale),
        out_shape=state,
        in_specs=[vmem] * 4,
        out_specs=[vmem] * 3,
        scratch_shapes=window(own),
        compiler_params=params,
        cost_estimate=light,
        name="own",
    )(nearer, queries, *own)
    kept = pl.pallas_call(
        functools.partial(join_kernel, scale, 0, False),
        out_shape=state,
        in_specs=[vmem] * 7,
        out_specs=[vmem] * 3,
        scratch_shapes=window(one),
        compiler_params=params,
        cost_estimate=light,
        name="one",
    )(nearer, queries, *kept, *one)
    return pl.pallas_call(
        functools.partial(join_kernel, scale, per_shard, True),
        out_shape=shape(queries.shape, queries.dtype),
        in_specs=[vmem] * (5 + len(far)),
        out_specs=pl.BlockSpec(memory_space=pl.ANY),
        scratch_shapes=window(far) + [pltpu.VMEM(queries.shape, queries.dtype), pltpu.SemaphoreType.DMA],
        compiler_params=params,
        cost_estimate=light,
        name="far",
    )(nearer, queries, *kept, *far)


def solution(mesh):
    in_specs = (
        P("ctx", "kvh", None),
        P(("ctx", "kvh"), None, None),
        P(("ctx", "kvh"), None, None),
        P(),
    )
    out_specs = P("ctx", "kvh", None)
    return jax.shard_map(body, mesh=mesh, in_specs=in_specs, out_specs=out_specs, check_vma=False)
```

```python
import functools
import math

import jax
import jax.numpy as jnp
from jax import lax
from jax.experimental import pallas as pl
from jax.experimental.pallas import tpu as pltpu
from jax.sharding import PartitionSpec as P

BLOCK = 128
CHUNK = 16
TOGETHER = 8
lowest = -1e30


def passed_along(piece, by, across=0, parity=None):
    shards, parts = lax.axis_size("ctx"), lax.axis_size("kvh")
    pairs = []
    for shard in range(shards):
        to = (shard + by) % shards if parity is None or shard % 2 == parity else shard ^ 1
        pairs += [(shard * parts + part, to * parts + (part ^ across)) for part in range(parts)]
    return lax.ppermute(piece, ("ctx", "kvh"), pairs)


def for_groups(pieces, me):
    pieces = pieces.reshape(2, 2, *pieces.shape[1:])
    pieces = jnp.where(me & 1 == 1, jnp.flip(pieces, 1), pieces)
    return jnp.where(me >> 1 == 1, jnp.flip(pieces, 0), pieces)


def plan_kernel(parts, longest, docs_ref, index_ref, spans_ref, last_ref, behind_ref):
    blocks = behind_ref.shape[0] - 1
    first = lax.div(index_ref[0], parts) * blocks
    spans, even, odd, start = jnp.int32(0), jnp.int32(0), jnp.int32(0), jnp.int32(0)
    behind = [jnp.int32(0)] * blocks
    for i in range(docs_ref.shape[0]):
        for block in range(blocks):
            behind[block] = jnp.where(first + block >= start, first + block - start, behind[block])
        end = start + docs_ref[i]
        head = lax.div(start, blocks)
        span = lax.div(end - 1, blocks) - head
        spans = jnp.maximum(spans, span)
        even = jnp.where((span >= longest) & (head % 2 == 0), 1, even)
        odd = jnp.where((span >= longest) & (head % 2 == 1), 2, odd)
        start = end
    spans_ref[0] = spans
    last_ref[0] = even + odd
    for row, number in enumerate((*behind, lax.rem(index_ref[0], parts))):
        behind_ref[row] = jnp.full(behind_ref.shape[1:], number, jnp.int32)


def fill(me, shard_refs, key_win, value_win, nearer=0):
    core, side = me & 1, me >> 1
    at = value_win.shape[0] - nearer * BLOCK
    for refs in shard_refs:
        at -= BLOCK * len(refs)
        for apart, ref in enumerate(refs):
            _, count, _, depth = ref.shape
            depth = depth // 2
            block = (side ^ apart) if len(refs) > 1 else 0
            rows = pl.ds(pl.multiple_of(at + block * BLOCK, BLOCK), BLOCK)
            for head in range(count):
                lanes = slice(head * depth, (head + 1) * depth)
                key, value = (
                    jnp.concatenate([ref[i ^ core, head, :, half] for i in range(2)], axis=0)
                    for half in (slice(0, depth), slice(depth, 2 * depth))
                )
                key_win[lanes, rows] = key.T
                value_win[rows, lanes] = value


def key_scores(count, heads, query, keys):
    head_of = lax.broadcasted_iota(jnp.int32, query.shape, 0) % heads // (heads // count)
    spread = jnp.concatenate(
        [jnp.where(head_of == head, query, jnp.zeros_like(query)) for head in range(count)], axis=1
    )
    return jnp.dot(spread, keys, preferred_element_type=jnp.float32)


def value_sums(count, heads, weights, values):
    wide = jnp.dot(weights.astype(jnp.bfloat16), values, preferred_element_type=jnp.float32)
    depth = wide.shape[1] // count
    tall = wide.reshape(wide.shape[0] // heads, count, heads // count, wide.shape[1])
    return jnp.concatenate(
        [tall[:, head : head + 1, :, head * depth : (head + 1) * depth] for head in range(count)], axis=1
    ).reshape(wide.shape[0], depth)


def lane_sums(weights):
    return sum(weights[:, at : at + BLOCK] for at in range(0, weights.shape[1], BLOCK))


def in_chunks(blocks, work):
    steps = BLOCK // CHUNK

    def together(some, carry):
        for step in range(TOGETHER):
            for block in range(blocks):
                work(block, some * TOGETHER + step)
        return carry

    if TOGETHER == steps:
        together(0, None)
    else:
        lax.fori_loop(0, steps // TOGETHER, together, None)


def own_kernel(scale, behind_ref, query_ref, *refs):
    *shard_refs, summed_ref, top_ref, total_ref, key_win, value_win = refs
    rows, heads, depth = query_ref.shape
    count = shard_refs[0].shape[1]
    blocks = rows // BLOCK
    *behind, me = [jnp.max(behind_ref[row]) for row in range(blocks + 1)]
    fill(me, [shard_refs], key_win, value_win)
    chunk_rows = CHUNK * heads
    ahead = lax.broadcasted_iota(jnp.int32, (chunk_rows, BLOCK), 1)
    ahead = ahead - lax.broadcasted_iota(jnp.int32, (chunk_rows, BLOCK), 0) // heads

    def work(numbers, block, step):
        start, width = (block - numbers[block]) * BLOCK, (numbers[block] + 1) * BLOCK
        first = block * BLOCK + step * CHUNK
        query = query_ref[pl.ds(first, CHUNK)].reshape(chunk_rows, depth)
        scores = key_scores(count, heads, query, key_win[:, start : start + width])
        last = jnp.where(ahead <= step * CHUNK, scores[:, width - BLOCK :], lowest)
        scores = jnp.concatenate([scores[:, : width - BLOCK], last], axis=1) if width > BLOCK else last
        top = jnp.max(scores, axis=1, keepdims=True)
        weights = jnp.exp2((scores - top) * (scale * math.log2(math.e)))
        at = pl.ds(pl.multiple_of(first * heads, chunk_rows), chunk_rows)
        top_ref[at] = jnp.broadcast_to(top, (chunk_rows, BLOCK))
        total_ref[at] = lane_sums(weights)
        summed_ref[at] = value_sums(count, heads, weights, value_win[start : start + width])

    joint = behind[1] >= 1 if blocks == 2 else None
    for same in (True, False):

        @pl.when(joint if same else jnp.logical_not(joint))
        def _():
            numbers = (0, int(same))
            in_chunks(blocks, functools.partial(work, numbers))


def join_kernel(scale, offset, final, behind_ref, query_ref, summed_in, top_in, total_in, *refs):
    outs = 1 if final else 3
    if final:
        extra = (len(refs) - 8) // 2
        shard_refs, rare_refs, refs = refs[:2], refs[2 : 2 + extra], refs[2 + extra :]
        out_to, key_win, value_win, out_ref, left, landed, *landing = refs
    else:
        shard_refs, (*out_refs, key_win, value_win) = refs[: -outs - 2], refs[-outs - 2 :]
    rows, heads, depth = query_ref.shape
    count = shard_refs[0].shape[1]
    groups = [shard_refs[i : i + 2] for i in range(0, len(shard_refs), 2)]
    blocks = rows // BLOCK
    window = value_win.shape[0] // BLOCK
    *behind, me = [jnp.max(behind_ref[row]) for row in range(blocks + 1)]
    fars = [jnp.clip(behind[block] - offset - block, 0, window) for block in range(blocks)]
    fill(me, groups, key_win, value_win)
    if final:

        @pl.when(jnp.maximum(*fars) > 2)
        def _():
            copies = [
                pltpu.make_async_copy(ref, to, landed.at[i]) for i, (ref, to) in enumerate(zip(rare_refs, landing))
            ]
            for copy in copies:
                copy.start()
            for copy in copies:
                copy.wait()
            rare = [landing[i : i + 2] for i in range(0, extra, 2)]
            fill(me, rare, key_win, value_win, 2)

    chunk_rows = CHUNK * heads
    rate = scale * math.log2(math.e)

    def work(taking, block, step):
        first = block * BLOCK + step * CHUNK
        at = pl.ds(pl.multiple_of(first * heads, chunk_rows), chunk_rows)
        if taking[block]:
            start = (window - taking[block]) * BLOCK
            query = query_ref[pl.ds(first, CHUNK)].reshape(chunk_rows, depth)
            scores = key_scores(count, heads, query, key_win[:, start:]) + hidden[block][:, start:]
            top_old = top_in[at]
            top = jnp.maximum(top_old, jnp.max(scores, axis=1, keepdims=True))
            fading = jnp.exp2((top_old - top) * rate)
            weights = jnp.exp2((scores - jnp.concatenate([top] * taking[block], axis=1)) * rate)
            total = total_in[at] * fading + lane_sums(weights)
            summed = summed_in[at] * fading + value_sums(count, heads, weights, value_win[start:])
        elif final:
            summed, total = summed_in[at], total_in[at]
        else:
            summed, top, total = summed_in[at], top_in[at], total_in[at]
        if final:
            out = (summed / jnp.sum(total, axis=1, keepdims=True)).astype(out_ref.dtype)
            out_ref[pl.ds(first, CHUNK)] = out.reshape(CHUNK, heads, depth)
            at = pl.ds(first, CHUNK)
            pltpu.make_async_copy(out_ref.at[at], out_to.at[at], left).start()
        else:
            for ref, value in zip(out_refs, (summed, top, total)):
                ref[at] = value

    column = lax.broadcasted_iota(jnp.int32, (1, window * BLOCK), 1)
    hidden = [jnp.where(column < (window - far) * BLOCK, lowest, 0.0) for far in fars]
    levels = sorted({0, min(2, window), window})
    even = window - window % 2
    cases = [(0, 0)] + [(n, m) for n in levels[1:] for m in sorted({0, 2, min(n, even)})]
    needed = [sum(jnp.where(far > low, high - low, 0) for low, high in zip(levels, levels[1:])) for far in fars]
    needed[1] = jnp.minimum(needed[1], even)
    for taking in cases:

        @pl.when(jnp.logical_and(needed[0] == taking[0], needed[1] == taking[1]))
        def _():
            in_chunks(blocks, functools.partial(work, taking))

    if final:
        pltpu.make_async_copy(out_ref, out_to, left).wait()


def body(queries, keys, values, doc_blocks):
    tokens, kv_heads, depth = keys.shape
    parts = lax.axis_size("kvh")
    count = kv_heads // parts
    rows, heads, _ = queries.shape
    sections = min(3, lax.axis_size("ctx") // 4)
    behind = 2**sections - 1
    per_shard = rows // BLOCK
    smem, vmem = pl.BlockSpec(memory_space=pltpu.SMEM), pl.BlockSpec(memory_space=pltpu.VMEM)
    params = pltpu.CompilerParams(vmem_limit_bytes=24 * 1024 * 1024)
    scale = 1.0 / math.sqrt(depth)
    light, medium = (
        pl.CostEstimate(flops=flops, bytes_accessed=2**20, transcendentals=10**6) for flops in (10**8, 10**9)
    )
    shape = jax.ShapeDtypeStruct
    me = lax.axis_index("kvh")
    index = (lax.axis_index("ctx") * parts + me).astype(jnp.int32).reshape(1)
    spans, last, nearer = pl.pallas_call(
        functools.partial(plan_kernel, parts, behind),
        cost_estimate=medium,
        out_shape=(shape((1,), jnp.int32), shape((1,), jnp.int32), shape((per_shard + 1, 8, 128), jnp.int32)),
        in_specs=[smem] * 2,
        out_specs=(smem, smem, vmem),
        name="plan",
    )(doc_blocks, index)
    both = lax.optimization_barrier(jnp.concatenate([keys, values], axis=2))
    both = both.reshape(tokens, parts, count, 2 * depth).transpose(1, 2, 0, 3)
    pieces = for_groups(both, me)
    swapped = passed_along(pieces[:, 1], 0, across=1)
    here, there = (jnp.stack([pieces[side, 0], swapped[side]]) for side in range(2))
    own = [here, passed_along(there, 0, across=2)]
    far = [passed_along(here, 2), passed_along(there, 2, across=2)]
    one = [passed_along(here, 1), passed_along(there, 1, across=2)]
    for distance in range(3, behind):
        send = functools.partial(passed_along, by=distance)
        far += [lax.cond(spans[0] >= distance, send, lambda x: x, x) for x in own]

    def late(parity):
        return lambda *halves: passed_along(jnp.where(me >= parts // 2, *halves), behind, parity=parity)

    far.append(lax.switch(last[0], [lambda *halves: halves[0], late(0), late(1), late(None)], *own))
    own, far[2:] = lax.optimization_barrier((own, far[2:]))

    state = [shape((rows * heads, depth), jnp.float32)] * 3

    def window(group):
        length = sum(s.shape[0] * s.shape[2] for s in group)
        return [
            pltpu.VMEM((count * depth, length), jnp.bfloat16),
            pltpu.VMEM((length, count * depth), jnp.bfloat16),
        ]

    kept = pl.pallas_call(
        functools.partial(own_kernel, scale),
        out_shape=state,
        in_specs=[vmem] * 4,
        out_specs=[vmem] * 3,
        scratch_shapes=window(own),
        compiler_params=params,
        cost_estimate=light,
        name="own",
    )(nearer, queries, *own)
    kept = pl.pallas_call(
        functools.partial(join_kernel, scale, 0, False),
        out_shape=state,
        in_specs=[vmem] * 7,
        out_specs=[vmem] * 3,
        scratch_shapes=window(one),
        compiler_params=params,
        cost_estimate=light,
        name="one",
    )(nearer, queries, *kept, *one)
    return pl.pallas_call(
        functools.partial(join_kernel, scale, per_shard, True),
        out_shape=shape(queries.shape, queries.dtype),
        in_specs=[vmem] * 7 + [pl.BlockSpec(memory_space=pl.ANY)] * (len(far) - 2),
        out_specs=pl.BlockSpec(memory_space=pl.ANY),
        scratch_shapes=[
            *window(far),
            pltpu.VMEM(queries.shape, queries.dtype),
            pltpu.SemaphoreType.DMA,
            pltpu.SemaphoreType.DMA((len(far) - 2,)),
            *[pltpu.VMEM(piece.shape, piece.dtype) for piece in far[2:]],
        ],
        compiler_params=params,
        cost_estimate=light,
        name="far",
    )(nearer, queries, *kept, *far)


def solution(mesh):
    in_specs = (
        P("ctx", "kvh", None),
        P(("ctx", "kvh"), None, None),
        P(("ctx", "kvh"), None, None),
        P(),
    )
    out_specs = P("ctx", "kvh", None)
    return jax.shard_map(body, mesh=mesh, in_specs=in_specs, out_specs=out_specs, check_vma=False)
```

```python
import functools
import math

import jax
import jax.numpy as jnp
from jax import lax
from jax.experimental import pallas as pl
from jax.experimental.pallas import tpu as pltpu
from jax.sharding import PartitionSpec as P

BLOCK = 128
CHUNK = 16
TOGETHER = 8
lowest = -1e30


def passed_along(piece, by, across=0, parity=None):
    shards, parts = lax.axis_size("ctx"), lax.axis_size("kvh")
    pairs = []
    for shard in range(shards):
        to = (shard + by) % shards if parity is None or shard % 2 == parity else shard ^ 1
        pairs += [(shard * parts + part, to * parts + (part ^ across)) for part in range(parts)]
    return lax.ppermute(piece, ("ctx", "kvh"), pairs)


def for_groups(pieces, me):
    pieces = pieces.reshape(2, 2, *pieces.shape[1:])
    pieces = jnp.where(me & 1 == 1, jnp.flip(pieces, 1), pieces)
    return jnp.where(me >> 1 == 1, jnp.flip(pieces, 0), pieces)


def plan_kernel(parts, longest, docs_ref, index_ref, spans_ref, last_ref, behind_ref):
    blocks = behind_ref.shape[0] - 1
    first = lax.div(index_ref[0], parts) * blocks
    spans, even, odd, start = jnp.int32(0), jnp.int32(0), jnp.int32(0), jnp.int32(0)
    behind = [jnp.int32(0)] * blocks
    for i in range(docs_ref.shape[0]):
        for block in range(blocks):
            behind[block] = jnp.where(first + block >= start, first + block - start, behind[block])
        end = start + docs_ref[i]
        head = lax.div(start, blocks)
        span = lax.div(end - 1, blocks) - head
        spans = jnp.maximum(spans, span)
        even = jnp.where((span >= longest) & (head % 2 == 0), 1, even)
        odd = jnp.where((span >= longest) & (head % 2 == 1), 2, odd)
        start = end
    spans_ref[0] = spans
    last_ref[0] = even + odd
    for row, number in enumerate((*behind, lax.rem(index_ref[0], parts))):
        behind_ref[row] = jnp.full(behind_ref.shape[1:], number, jnp.int32)


def fill(me, shard_refs, key_win, value_win, nearer=0):
    core, side = me & 1, me >> 1
    at = value_win.shape[0] - nearer * BLOCK
    for refs in shard_refs:
        at -= BLOCK * len(refs)
        for apart, ref in enumerate(refs):
            _, count, _, depth = ref.shape
            depth = depth // 2
            block = (side ^ apart) if len(refs) > 1 else 0
            rows = pl.ds(pl.multiple_of(at + block * BLOCK, BLOCK), BLOCK)
            for head in range(count):
                lanes = slice(head * depth, (head + 1) * depth)
                key, value = (
                    jnp.concatenate([ref[i ^ core, head, :, half] for i in range(2)], axis=0)
                    for half in (slice(0, depth), slice(depth, 2 * depth))
                )
                key_win[lanes, rows] = key.T
                value_win[rows, lanes] = value


def key_scores(count, heads, query, keys):
    head_of = lax.broadcasted_iota(jnp.int32, query.shape, 0) % heads // (heads // count)
    spread = jnp.concatenate(
        [jnp.where(head_of == head, query, jnp.zeros_like(query)) for head in range(count)], axis=1
    )
    return jnp.dot(spread, keys, preferred_element_type=jnp.float32)


def value_sums(count, heads, weights, values):
    wide = jnp.dot(weights.astype(jnp.bfloat16), values, preferred_element_type=jnp.float32)
    depth = wide.shape[1] // count
    tall = wide.reshape(wide.shape[0] // heads, count, heads // count, wide.shape[1])
    return jnp.concatenate(
        [tall[:, head : head + 1, :, head * depth : (head + 1) * depth] for head in range(count)], axis=1
    ).reshape(wide.shape[0], depth)


def lane_sums(weights):
    return sum(weights[:, at : at + BLOCK] for at in range(0, weights.shape[1], BLOCK))


def in_chunks(blocks, work):
    steps = BLOCK // CHUNK

    def together(some, carry):
        for step in range(TOGETHER):
            for block in range(blocks):
                work(block, some * TOGETHER + step)
        return carry

    if TOGETHER == steps:
        together(0, None)
    else:
        lax.fori_loop(0, steps // TOGETHER, together, None)


def own_kernel(scale, behind_ref, query_ref, *refs):
    *shard_refs, summed_ref, top_ref, total_ref, key_win, value_win = refs
    rows, heads, depth = query_ref.shape
    count = shard_refs[0].shape[1]
    blocks = rows // BLOCK
    *behind, me = [jnp.max(behind_ref[row]) for row in range(blocks + 1)]
    fill(me, [shard_refs], key_win, value_win)
    chunk_rows = CHUNK * heads
    ahead = lax.broadcasted_iota(jnp.int32, (chunk_rows, BLOCK), 1)
    ahead = ahead - lax.broadcasted_iota(jnp.int32, (chunk_rows, BLOCK), 0) // heads

    def work(numbers, block, step):
        start, width = (block - numbers[block]) * BLOCK, (numbers[block] + 1) * BLOCK
        first = block * BLOCK + step * CHUNK
        query = query_ref[pl.ds(first, CHUNK)].reshape(chunk_rows, depth)
        scores = key_scores(count, heads, query, key_win[:, start : start + width])
        last = jnp.where(ahead <= step * CHUNK, scores[:, width - BLOCK :], lowest)
        scores = jnp.concatenate([scores[:, : width - BLOCK], last], axis=1) if width > BLOCK else last
        top = jnp.max(scores, axis=1, keepdims=True)
        weights = jnp.exp2((scores - top) * (scale * math.log2(math.e)))
        at = pl.ds(pl.multiple_of(first * heads, chunk_rows), chunk_rows)
        top_ref[at] = jnp.broadcast_to(top, (chunk_rows, BLOCK))
        total_ref[at] = lane_sums(weights)
        summed_ref[at] = value_sums(count, heads, weights, value_win[start : start + width])

    joint = behind[1] >= 1 if blocks == 2 else None
    for same in (True, False):

        @pl.when(joint if same else jnp.logical_not(joint))
        def _():
            numbers = (0, int(same))
            in_chunks(blocks, functools.partial(work, numbers))


def join_kernel(scale, offset, final, behind_ref, query_ref, summed_in, top_in, total_in, *refs):
    outs = 1 if final else 3
    if final:
        extra = (len(refs) - 8) // 2
        shard_refs, rare_refs, refs = refs[:2], refs[2 : 2 + extra], refs[2 + extra :]
        out_to, key_win, value_win, out_ref, left, landed, *landing = refs
    else:
        shard_refs, (*out_refs, key_win, value_win) = refs[: -outs - 2], refs[-outs - 2 :]
    rows, heads, depth = query_ref.shape
    count = shard_refs[0].shape[1]
    groups = [shard_refs[i : i + 2] for i in range(0, len(shard_refs), 2)]
    blocks = rows // BLOCK
    window = value_win.shape[0] // BLOCK
    *behind, me = [jnp.max(behind_ref[row]) for row in range(blocks + 1)]
    fars = [jnp.clip(behind[block] - offset - block, 0, window) for block in range(blocks)]
    fill(me, groups, key_win, value_win)
    if final:

        @pl.when(jnp.maximum(*fars) > 2)
        def _():
            copies = [
                pltpu.make_async_copy(ref, to, landed.at[i]) for i, (ref, to) in enumerate(zip(rare_refs, landing))
            ]
            for copy in copies:
                copy.start()
            for copy in copies:
                copy.wait()
            rare = [landing[i : i + 2] for i in range(0, extra, 2)]
            fill(me, rare, key_win, value_win, 2)

    chunk_rows = CHUNK * heads
    rate = scale * math.log2(math.e)

    def work(taking, block, step):
        first = block * BLOCK + step * CHUNK
        at = pl.ds(pl.multiple_of(first * heads, chunk_rows), chunk_rows)
        if taking[block]:
            start = (window - taking[block]) * BLOCK
            query = query_ref[pl.ds(first, CHUNK)].reshape(chunk_rows, depth)
            scores = key_scores(count, heads, query, key_win[:, start:]) + hidden[block][:, start:]
            top_old = top_in[at]
            top = jnp.maximum(top_old, jnp.max(scores, axis=1, keepdims=True))
            fading = jnp.exp2((top_old - top) * rate)
            weights = jnp.exp2((scores - jnp.concatenate([top] * taking[block], axis=1)) * rate)
            total = total_in[at] * fading + lane_sums(weights)
            summed = summed_in[at] * fading + value_sums(count, heads, weights, value_win[start:])
        elif final:
            summed, total = summed_in[at], total_in[at]
        else:
            summed, top, total = summed_in[at], top_in[at], total_in[at]
        if final:
            out = (summed / jnp.sum(total, axis=1, keepdims=True)).astype(out_ref.dtype)
            out_ref[pl.ds(first, CHUNK)] = out.reshape(CHUNK, heads, depth)
            at = pl.ds(first, CHUNK)
            pltpu.make_async_copy(out_ref.at[at], out_to.at[at], left).start()
        else:
            for ref, value in zip(out_refs, (summed, top, total)):
                ref[at] = value

    column = lax.broadcasted_iota(jnp.int32, (1, window * BLOCK), 1)
    hidden = [jnp.where(column < (window - far) * BLOCK, lowest, 0.0) for far in fars]
    levels = sorted({0, min(2, window), window})
    even = window - window % 2
    cases = [(0, 0)] + [(n, m) for n in levels[1:] for m in sorted({0, 2, min(n, even)})]
    needed = [sum(jnp.where(far > low, high - low, 0) for low, high in zip(levels, levels[1:])) for far in fars]
    needed[1] = jnp.minimum(needed[1], even)
    for taking in cases:

        @pl.when(jnp.logical_and(needed[0] == taking[0], needed[1] == taking[1]))
        def _():
            in_chunks(blocks, functools.partial(work, taking))

    if final:
        pltpu.make_async_copy(out_ref, out_to, left).wait()


def body(queries, keys, values, doc_blocks):
    tokens, kv_heads, depth = keys.shape
    parts = lax.axis_size("kvh")
    count = kv_heads // parts
    rows, heads, _ = queries.shape
    sections = min(3, lax.axis_size("ctx") // 4)
    behind = 2**sections - 1
    per_shard = rows // BLOCK
    smem, vmem = pl.BlockSpec(memory_space=pltpu.SMEM), pl.BlockSpec(memory_space=pltpu.VMEM)
    params = pltpu.CompilerParams(vmem_limit_bytes=24 * 1024 * 1024)
    scale = 1.0 / math.sqrt(depth)
    light, medium = (
        pl.CostEstimate(flops=flops, bytes_accessed=2**20, transcendentals=10**6) for flops in (10**9, 10**9)
    )
    shape = jax.ShapeDtypeStruct
    me = lax.axis_index("kvh")
    index = (lax.axis_index("ctx") * parts + me).astype(jnp.int32).reshape(1)
    spans, last, nearer = pl.pallas_call(
        functools.partial(plan_kernel, parts, behind),
        cost_estimate=medium,
        out_shape=(shape((1,), jnp.int32), shape((1,), jnp.int32), shape((per_shard + 1, 8, 128), jnp.int32)),
        in_specs=[smem] * 2,
        out_specs=(smem, smem, vmem),
        name="plan",
    )(doc_blocks, index)
    both = lax.optimization_barrier(jnp.concatenate([keys, values], axis=2))
    both = both.reshape(tokens, parts, count, 2 * depth).transpose(1, 2, 0, 3)
    pieces = for_groups(both, me)
    swapped = passed_along(pieces[:, 1], 0, across=1)
    here, there = (jnp.stack([pieces[side, 0], swapped[side]]) for side in range(2))
    own = [here, passed_along(there, 0, across=2)]
    far = [passed_along(here, 2), passed_along(there, 2, across=2)]
    one = [passed_along(here, 1), passed_along(there, 1, across=2)]
    for distance in range(3, behind):
        send = functools.partial(passed_along, by=distance)
        far += [lax.cond(spans[0] >= distance, send, lambda x: x, x) for x in own]

    def late(parity):
        return lambda *halves: passed_along(jnp.where(me >= parts // 2, *halves), behind, parity=parity)

    far.append(lax.switch(last[0], [lambda *halves: halves[0], late(0), late(1), late(None)], *own))
    own, far[2:] = lax.optimization_barrier((own, far[2:]))

    state = [shape((rows * heads, depth), jnp.float32)] * 3

    def window(group):
        length = sum(s.shape[0] * s.shape[2] for s in group)
        return [
            pltpu.VMEM((count * depth, length), jnp.bfloat16),
            pltpu.VMEM((length, count * depth), jnp.bfloat16),
        ]

    kept = pl.pallas_call(
        functools.partial(own_kernel, scale),
        out_shape=state,
        in_specs=[vmem] * 4,
        out_specs=[vmem] * 3,
        scratch_shapes=window(own),
        compiler_params=params,
        cost_estimate=light,
        name="own",
    )(nearer, queries, *own)
    kept = pl.pallas_call(
        functools.partial(join_kernel, scale, 0, False),
        out_shape=state,
        in_specs=[vmem] * 7,
        out_specs=[vmem] * 3,
        scratch_shapes=window(one),
        compiler_params=params,
        cost_estimate=light,
        name="one",
    )(nearer, queries, *kept, *one)
    return pl.pallas_call(
        functools.partial(join_kernel, scale, per_shard, True),
        out_shape=shape(queries.shape, queries.dtype),
        in_specs=[vmem] * 7 + [pl.BlockSpec(memory_space=pl.ANY)] * (len(far) - 2),
        out_specs=pl.BlockSpec(memory_space=pl.ANY),
        scratch_shapes=[
            *window(far),
            pltpu.VMEM(queries.shape, queries.dtype),
            pltpu.SemaphoreType.DMA,
            pltpu.SemaphoreType.DMA((len(far) - 2,)),
            *[pltpu.VMEM(piece.shape, piece.dtype) for piece in far[2:]],
        ],
        compiler_params=params,
        cost_estimate=light,
        name="far",
    )(nearer, queries, *kept, *far)


def solution(mesh):
    in_specs = (
        P("ctx", "kvh", None),
        P(("ctx", "kvh"), None, None),
        P(("ctx", "kvh"), None, None),
        P(),
    )
    out_specs = P("ctx", "kvh", None)
    return jax.shard_map(body, mesh=mesh, in_specs=in_specs, out_specs=out_specs, check_vma=False)
```

```python
import functools
import math

import jax
import jax.numpy as jnp
from jax import lax
from jax.experimental import pallas as pl
from jax.experimental.pallas import tpu as pltpu
from jax.sharding import PartitionSpec as P

BLOCK = 128
CHUNK = 16
TOGETHER = 8
lowest = -1e30


def passed_along(piece, by, across=0, parity=None):
    shards, parts = lax.axis_size("ctx"), lax.axis_size("kvh")
    pairs = []
    for shard in range(shards):
        to = (shard + by) % shards if parity is None or shard % 2 == parity else shard ^ 1
        pairs += [(shard * parts + part, to * parts + (part ^ across)) for part in range(parts)]
    return lax.ppermute(piece, ("ctx", "kvh"), pairs)


def for_groups(pieces, me):
    pieces = pieces.reshape(2, 2, *pieces.shape[1:])
    pieces = jnp.where(me & 1 == 1, jnp.flip(pieces, 1), pieces)
    return jnp.where(me >> 1 == 1, jnp.flip(pieces, 0), pieces)


def plan_kernel(parts, longest, docs_ref, index_ref, spans_ref, last_ref, behind_ref):
    blocks = behind_ref.shape[0] - 1
    first = lax.div(index_ref[0], parts) * blocks
    spans, even, odd, start = jnp.int32(0), jnp.int32(0), jnp.int32(0), jnp.int32(0)
    behind = [jnp.int32(0)] * blocks
    for i in range(docs_ref.shape[0]):
        for block in range(blocks):
            behind[block] = jnp.where(first + block >= start, first + block - start, behind[block])
        end = start + docs_ref[i]
        head = lax.div(start, blocks)
        span = lax.div(end - 1, blocks) - head
        spans = jnp.maximum(spans, span)
        even = jnp.where((span >= longest) & (head % 2 == 0), 1, even)
        odd = jnp.where((span >= longest) & (head % 2 == 1), 2, odd)
        start = end
    spans_ref[0] = spans
    last_ref[0] = even + odd
    for row, number in enumerate((*behind, lax.rem(index_ref[0], parts))):
        behind_ref[row] = jnp.full(behind_ref.shape[1:], number, jnp.int32)


def fill(me, shard_refs, key_win, value_win, nearer=0):
    core, side = me & 1, me >> 1
    at = value_win.shape[0] - nearer * BLOCK
    for refs in shard_refs:
        at -= BLOCK * len(refs)
        for apart, ref in enumerate(refs):
            _, count, _, depth = ref.shape
            depth = depth // 2
            block = (side ^ apart) if len(refs) > 1 else 0
            rows = pl.ds(pl.multiple_of(at + block * BLOCK, BLOCK), BLOCK)
            for head in range(count):
                lanes = slice(head * depth, (head + 1) * depth)
                key, value = (
                    jnp.concatenate([ref[i ^ core, head, :, half] for i in range(2)], axis=0)
                    for half in (slice(0, depth), slice(depth, 2 * depth))
                )
                key_win[lanes, rows] = key.T
                value_win[rows, lanes] = value


def key_scores(count, heads, query, keys):
    head_of = lax.broadcasted_iota(jnp.int32, query.shape, 0) % heads // (heads // count)
    spread = jnp.concatenate(
        [jnp.where(head_of == head, query, jnp.zeros_like(query)) for head in range(count)], axis=1
    )
    return jnp.dot(spread, keys, preferred_element_type=jnp.float32)


def value_sums(count, heads, weights, values):
    wide = jnp.dot(weights.astype(jnp.bfloat16), values, preferred_element_type=jnp.float32)
    depth = wide.shape[1] // count
    tall = wide.reshape(wide.shape[0] // heads, count, heads // count, wide.shape[1])
    return jnp.concatenate(
        [tall[:, head : head + 1, :, head * depth : (head + 1) * depth] for head in range(count)], axis=1
    ).reshape(wide.shape[0], depth)


def lane_sums(weights):
    return sum(weights[:, at : at + BLOCK] for at in range(0, weights.shape[1], BLOCK))


def in_chunks(blocks, work):
    steps = BLOCK // CHUNK

    def together(some, carry):
        for step in range(TOGETHER):
            for block in range(blocks):
                work(block, some * TOGETHER + step)
        return carry

    if TOGETHER == steps:
        together(0, None)
    else:
        lax.fori_loop(0, steps // TOGETHER, together, None)


def own_kernel(scale, behind_ref, query_ref, *refs):
    *shard_refs, summed_ref, top_ref, total_ref, key_win, value_win = refs
    rows, heads, depth = query_ref.shape
    count = shard_refs[0].shape[1]
    blocks = rows // BLOCK
    *behind, me = [jnp.max(behind_ref[row]) for row in range(blocks + 1)]
    fill(me, [shard_refs], key_win, value_win)
    chunk_rows = CHUNK * heads
    ahead = lax.broadcasted_iota(jnp.int32, (chunk_rows, BLOCK), 1)
    ahead = ahead - lax.broadcasted_iota(jnp.int32, (chunk_rows, BLOCK), 0) // heads

    def work(numbers, block, step):
        start, width = (block - numbers[block]) * BLOCK, (numbers[block] + 1) * BLOCK
        first = block * BLOCK + step * CHUNK
        query = query_ref[pl.ds(first, CHUNK)].reshape(chunk_rows, depth)
        scores = key_scores(count, heads, query, key_win[:, start : start + width])
        last = jnp.where(ahead <= step * CHUNK, scores[:, width - BLOCK :], lowest)
        scores = jnp.concatenate([scores[:, : width - BLOCK], last], axis=1) if width > BLOCK else last
        top = jnp.max(scores, axis=1, keepdims=True)
        weights = jnp.exp2((scores - top) * (scale * math.log2(math.e)))
        at = pl.ds(pl.multiple_of(first * heads, chunk_rows), chunk_rows)
        top_ref[at] = jnp.broadcast_to(top, (chunk_rows, BLOCK))
        total_ref[at] = lane_sums(weights)
        summed_ref[at] = value_sums(count, heads, weights, value_win[start : start + width])

    joint = behind[1] >= 1 if blocks == 2 else None
    for same in (True, False):

        @pl.when(joint if same else jnp.logical_not(joint))
        def _():
            numbers = (0, int(same))
            in_chunks(blocks, functools.partial(work, numbers))


def join_kernel(scale, offset, final, behind_ref, query_ref, summed_in, top_in, total_in, *refs):
    outs = 1 if final else 3
    if final:
        extra = (len(refs) - 8) // 2
        shard_refs, rare_refs, refs = refs[:2], refs[2 : 2 + extra], refs[2 + extra :]
        out_to, key_win, value_win, out_ref, left, landed, *landing = refs
    else:
        shard_refs, (*out_refs, key_win, value_win) = refs[: -outs - 2], refs[-outs - 2 :]
    rows, heads, depth = query_ref.shape
    count = shard_refs[0].shape[1]
    groups = [shard_refs[i : i + 2] for i in range(0, len(shard_refs), 2)]
    blocks = rows // BLOCK
    window = value_win.shape[0] // BLOCK
    *behind, me = [jnp.max(behind_ref[row]) for row in range(blocks + 1)]
    fars = [jnp.clip(behind[block] - offset - block, 0, window) for block in range(blocks)]
    fill(me, groups, key_win, value_win)
    if final:

        @pl.when(jnp.maximum(*fars) > 2)
        def _():
            copies = [
                pltpu.make_async_copy(ref, to, landed.at[i]) for i, (ref, to) in enumerate(zip(rare_refs, landing))
            ]
            for copy in copies:
                copy.start()
            for copy in copies:
                copy.wait()
            rare = [landing[i : i + 2] for i in range(0, extra, 2)]
            fill(me, rare, key_win, value_win, 2)

    chunk_rows = CHUNK * heads
    rate = scale * math.log2(math.e)

    def work(taking, block, step):
        first = block * BLOCK + step * CHUNK
        at = pl.ds(pl.multiple_of(first * heads, chunk_rows), chunk_rows)
        if taking[block]:
            start = (window - taking[block]) * BLOCK
            query = query_ref[pl.ds(first, CHUNK)].reshape(chunk_rows, depth)
            scores = key_scores(count, heads, query, key_win[:, start:]) + hidden[block][:, start:]
            top_old = top_in[at]
            top = jnp.maximum(top_old, jnp.max(scores, axis=1, keepdims=True))
            fading = jnp.exp2((top_old - top) * rate)
            weights = jnp.exp2((scores - jnp.concatenate([top] * taking[block], axis=1)) * rate)
            total = total_in[at] * fading + lane_sums(weights)
            summed = summed_in[at] * fading + value_sums(count, heads, weights, value_win[start:])
        elif final:
            summed, total = summed_in[at], total_in[at]
        else:
            summed, top, total = summed_in[at], top_in[at], total_in[at]
        if final:
            out = (summed / jnp.sum(total, axis=1, keepdims=True)).astype(out_ref.dtype)
            out_ref[pl.ds(first, CHUNK)] = out.reshape(CHUNK, heads, depth)
            at = pl.ds(first, CHUNK)
            pltpu.make_async_copy(out_ref.at[at], out_to.at[at], left).start()
        else:
            for ref, value in zip(out_refs, (summed, top, total)):
                ref[at] = value

    column = lax.broadcasted_iota(jnp.int32, (1, window * BLOCK), 1)
    hidden = [jnp.where(column < (window - far) * BLOCK, lowest, 0.0) for far in fars]
    levels = sorted({0, min(2, window), window})
    even = window - window % 2
    cases = [(0, 0)] + [(n, m) for n in levels[1:] for m in sorted({0, 2, min(n, even)})]
    needed = [sum(jnp.where(far > low, high - low, 0) for low, high in zip(levels, levels[1:])) for far in fars]
    needed[1] = jnp.minimum(needed[1], even)
    for taking in cases:

        @pl.when(jnp.logical_and(needed[0] == taking[0], needed[1] == taking[1]))
        def _():
            in_chunks(blocks, functools.partial(work, taking))

    if final:
        pltpu.make_async_copy(out_ref, out_to, left).wait()


def body(queries, keys, values, doc_blocks):
    tokens, kv_heads, depth = keys.shape
    parts = lax.axis_size("kvh")
    count = kv_heads // parts
    rows, heads, _ = queries.shape
    sections = min(3, lax.axis_size("ctx") // 4)
    behind = 2**sections - 1
    per_shard = rows // BLOCK
    smem, vmem = pl.BlockSpec(memory_space=pltpu.SMEM), pl.BlockSpec(memory_space=pltpu.VMEM)
    params = pltpu.CompilerParams(vmem_limit_bytes=24 * 1024 * 1024)
    scale = 1.0 / math.sqrt(depth)
    light, medium = (
        pl.CostEstimate(flops=flops, bytes_accessed=2**20, transcendentals=10**6) for flops in (10**8, 10**9)
    )
    shape = jax.ShapeDtypeStruct
    me = lax.axis_index("kvh")
    index = (lax.axis_index("ctx") * parts + me).astype(jnp.int32).reshape(1)
    spans, last, nearer = pl.pallas_call(
        functools.partial(plan_kernel, parts, behind),
        cost_estimate=medium,
        out_shape=(shape((1,), jnp.int32), shape((1,), jnp.int32), shape((per_shard + 1, 8, 128), jnp.int32)),
        in_specs=[smem] * 2,
        out_specs=(smem, smem, vmem),
        name="plan",
    )(doc_blocks, index)
    both = lax.optimization_barrier(jnp.concatenate([keys, values], axis=2))
    both = both.reshape(tokens, parts, count, 2 * depth).transpose(1, 2, 0, 3)
    pieces = for_groups(both, me)
    swapped = passed_along(pieces[:, 1], 0, across=1)
    swapped, spans, last, nearer = lax.optimization_barrier((swapped, spans, last, nearer))
    here, there = (jnp.stack([pieces[side, 0], swapped[side]]) for side in range(2))
    own = [here, passed_along(there, 0, across=2)]
    far = [passed_along(here, 2), passed_along(there, 2, across=2)]
    one = [passed_along(here, 1), passed_along(there, 1, across=2)]
    for distance in range(3, behind):
        send = functools.partial(passed_along, by=distance)
        far += [lax.cond(spans[0] >= distance, send, lambda x: x, x) for x in own]

    def late(parity):
        return lambda *halves: passed_along(jnp.where(me >= parts // 2, *halves), behind, parity=parity)

    far.append(lax.switch(last[0], [lambda *halves: halves[0], late(0), late(1), late(None)], *own))
    own, far[2:] = lax.optimization_barrier((own, far[2:]))

    state = [shape((rows * heads, depth), jnp.float32)] * 3

    def window(group):
        length = sum(s.shape[0] * s.shape[2] for s in group)
        return [
            pltpu.VMEM((count * depth, length), jnp.bfloat16),
            pltpu.VMEM((length, count * depth), jnp.bfloat16),
        ]

    kept = pl.pallas_call(
        functools.partial(own_kernel, scale),
        out_shape=state,
        in_specs=[vmem] * 4,
        out_specs=[vmem] * 3,
        scratch_shapes=window(own),
        compiler_params=params,
        cost_estimate=light,
        name="own",
    )(nearer, queries, *own)
    kept = pl.pallas_call(
        functools.partial(join_kernel, scale, 0, False),
        out_shape=state,
        in_specs=[vmem] * 7,
        out_specs=[vmem] * 3,
        scratch_shapes=window(one),
        compiler_params=params,
        cost_estimate=light,
        name="one",
    )(nearer, queries, *kept, *one)
    return pl.pallas_call(
        functools.partial(join_kernel, scale, per_shard, True),
        out_shape=shape(queries.shape, queries.dtype),
        in_specs=[vmem] * 7 + [pl.BlockSpec(memory_space=pl.ANY)] * (len(far) - 2),
        out_specs=pl.BlockSpec(memory_space=pl.ANY),
        scratch_shapes=[
            *window(far),
            pltpu.VMEM(queries.shape, queries.dtype),
            pltpu.SemaphoreType.DMA,
            pltpu.SemaphoreType.DMA((len(far) - 2,)),
            *[pltpu.VMEM(piece.shape, piece.dtype) for piece in far[2:]],
        ],
        compiler_params=params,
        cost_estimate=light,
        name="far",
    )(nearer, queries, *kept, *far)


def solution(mesh):
    in_specs = (
        P("ctx", "kvh", None),
        P(("ctx", "kvh"), None, None),
        P(("ctx", "kvh"), None, None),
        P(),
    )
    out_specs = P("ctx", "kvh", None)
    return jax.shard_map(body, mesh=mesh, in_specs=in_specs, out_specs=out_specs, check_vma=False)
```

```python
import functools
import math

import jax
import jax.numpy as jnp
from jax import lax
from jax.experimental import pallas as pl
from jax.experimental.pallas import tpu as pltpu
from jax.sharding import PartitionSpec as P

BLOCK = 128
CHUNK = 16
TOGETHER = 8
lowest = -1e30


def passed_along(piece, by, across=0, parity=None):
    shards, parts = lax.axis_size("ctx"), lax.axis_size("kvh")
    pairs = []
    for shard in range(shards):
        to = (shard + by) % shards if parity is None or shard % 2 == parity else shard ^ 1
        pairs += [(shard * parts + part, to * parts + (part ^ across)) for part in range(parts)]
    return lax.ppermute(piece, ("ctx", "kvh"), pairs)


def for_groups(pieces, me):
    pieces = pieces.reshape(2, 2, *pieces.shape[1:])
    pieces = jnp.where(me & 1 == 1, jnp.flip(pieces, 1), pieces)
    return jnp.where(me >> 1 == 1, jnp.flip(pieces, 0), pieces)


def plan_kernel(parts, longest, docs_ref, index_ref, spans_ref, last_ref, behind_ref):
    blocks = behind_ref.shape[0] - 1
    first = lax.div(index_ref[0], parts) * blocks
    spans, even, odd, start = jnp.int32(0), jnp.int32(0), jnp.int32(0), jnp.int32(0)
    behind = [jnp.int32(0)] * blocks
    for i in range(docs_ref.shape[0]):
        for block in range(blocks):
            behind[block] = jnp.where(first + block >= start, first + block - start, behind[block])
        end = start + docs_ref[i]
        head = lax.div(start, blocks)
        span = lax.div(end - 1, blocks) - head
        spans = jnp.maximum(spans, span)
        even = jnp.where((span >= longest) & (head % 2 == 0), 1, even)
        odd = jnp.where((span >= longest) & (head % 2 == 1), 2, odd)
        start = end
    spans_ref[0] = spans
    last_ref[0] = even + odd
    for row, number in enumerate((*behind, lax.rem(index_ref[0], parts))):
        behind_ref[row] = jnp.full(behind_ref.shape[1:], number, jnp.int32)


def fill(me, shard_refs, key_win, value_win, nearer=0):
    core, side = me & 1, me >> 1
    at = value_win.shape[0] - nearer * BLOCK
    for refs in shard_refs:
        at -= BLOCK * len(refs)
        for apart, ref in enumerate(refs):
            _, count, _, depth = ref.shape
            depth = depth // 2
            block = (side ^ apart) if len(refs) > 1 else 0
            rows = pl.ds(pl.multiple_of(at + block * BLOCK, BLOCK), BLOCK)
            for head in range(count):
                lanes = slice(head * depth, (head + 1) * depth)
                key, value = (
                    jnp.concatenate([ref[i ^ core, head, :, half] for i in range(2)], axis=0)
                    for half in (slice(0, depth), slice(depth, 2 * depth))
                )
                key_win[lanes, rows] = key.T
                value_win[rows, lanes] = value


def key_scores(count, heads, query, keys):
    head_of = lax.broadcasted_iota(jnp.int32, query.shape, 0) % heads // (heads // count)
    spread = jnp.concatenate(
        [jnp.where(head_of == head, query, jnp.zeros_like(query)) for head in range(count)], axis=1
    )
    return jnp.dot(spread, keys, preferred_element_type=jnp.float32)


def value_sums(count, heads, weights, values):
    wide = jnp.dot(weights.astype(jnp.bfloat16), values, preferred_element_type=jnp.float32)
    depth = wide.shape[1] // count
    tall = wide.reshape(wide.shape[0] // heads, count, heads // count, wide.shape[1])
    return jnp.concatenate(
        [tall[:, head : head + 1, :, head * depth : (head + 1) * depth] for head in range(count)], axis=1
    ).reshape(wide.shape[0], depth)


def lane_sums(weights):
    return sum(weights[:, at : at + BLOCK] for at in range(0, weights.shape[1], BLOCK))


def in_chunks(blocks, work):
    steps = BLOCK // CHUNK

    def together(some, carry):
        for step in range(TOGETHER):
            for block in range(blocks):
                work(block, some * TOGETHER + step)
        return carry

    if TOGETHER == steps:
        together(0, None)
    else:
        lax.fori_loop(0, steps // TOGETHER, together, None)


def own_kernel(scale, behind_ref, query_ref, *refs):
    *shard_refs, summed_ref, top_ref, total_ref, key_win, value_win = refs
    rows, heads, depth = query_ref.shape
    count = shard_refs[0].shape[1]
    blocks = rows // BLOCK
    *behind, me = [jnp.max(behind_ref[row]) for row in range(blocks + 1)]
    fill(me, [shard_refs], key_win, value_win)
    chunk_rows = CHUNK * heads
    ahead = lax.broadcasted_iota(jnp.int32, (chunk_rows, BLOCK), 1)
    ahead = ahead - lax.broadcasted_iota(jnp.int32, (chunk_rows, BLOCK), 0) // heads

    def work(numbers, block, step):
        start, width = (block - numbers[block]) * BLOCK, (numbers[block] + 1) * BLOCK
        first = block * BLOCK + step * CHUNK
        query = query_ref[pl.ds(first, CHUNK)].reshape(chunk_rows, depth)
        scores = key_scores(count, heads, query, key_win[:, start : start + width])
        last = jnp.where(ahead <= step * CHUNK, scores[:, width - BLOCK :], lowest)
        scores = jnp.concatenate([scores[:, : width - BLOCK], last], axis=1) if width > BLOCK else last
        top = jnp.max(scores, axis=1, keepdims=True)
        weights = jnp.exp2((scores - top) * (scale * math.log2(math.e)))
        at = pl.ds(pl.multiple_of(first * heads, chunk_rows), chunk_rows)
        top_ref[at] = jnp.broadcast_to(top, (chunk_rows, BLOCK))
        total_ref[at] = lane_sums(weights)
        summed_ref[at] = value_sums(count, heads, weights, value_win[start : start + width])

    joint = behind[1] >= 1 if blocks == 2 else None
    for same in (True, False):

        @pl.when(joint if same else jnp.logical_not(joint))
        def _():
            numbers = (0, int(same))
            in_chunks(blocks, functools.partial(work, numbers))


def join_kernel(scale, offset, final, behind_ref, query_ref, summed_in, top_in, total_in, *refs):
    outs = 1 if final else 3
    if final:
        extra = (len(refs) - 8) // 2
        shard_refs, rare_refs, refs = refs[:2], refs[2 : 2 + extra], refs[2 + extra :]
        out_to, key_win, value_win, out_ref, left, landed, *landing = refs
    else:
        shard_refs, (*out_refs, key_win, value_win) = refs[: -outs - 2], refs[-outs - 2 :]
    rows, heads, depth = query_ref.shape
    count = shard_refs[0].shape[1]
    groups = [shard_refs[i : i + 2] for i in range(0, len(shard_refs), 2)]
    blocks = rows // BLOCK
    window = value_win.shape[0] // BLOCK
    *behind, me = [jnp.max(behind_ref[row]) for row in range(blocks + 1)]
    fars = [jnp.clip(behind[block] - offset - block, 0, window) for block in range(blocks)]
    fill(me, groups, key_win, value_win)
    if final:

        @pl.when(jnp.maximum(*fars) > 2)
        def _():
            copies = [
                pltpu.make_async_copy(ref, to, landed.at[i]) for i, (ref, to) in enumerate(zip(rare_refs, landing))
            ]
            for copy in copies:
                copy.start()
            for copy in copies:
                copy.wait()
            rare = [landing[i : i + 2] for i in range(0, extra, 2)]
            fill(me, rare, key_win, value_win, 2)

    chunk_rows = CHUNK * heads
    rate = scale * math.log2(math.e)

    def work(taking, block, step):
        first = block * BLOCK + step * CHUNK
        at = pl.ds(pl.multiple_of(first * heads, chunk_rows), chunk_rows)
        if taking[block]:
            start = (window - taking[block]) * BLOCK
            query = query_ref[pl.ds(first, CHUNK)].reshape(chunk_rows, depth)
            scores = key_scores(count, heads, query, key_win[:, start:]) + hidden[block][:, start:]
            top_old = top_in[at]
            top = jnp.maximum(top_old, jnp.max(scores, axis=1, keepdims=True))
            fading = jnp.exp2((top_old - top) * rate)
            weights = jnp.exp2((scores - jnp.concatenate([top] * taking[block], axis=1)) * rate)
            total = total_in[at] * fading + lane_sums(weights)
            summed = summed_in[at] * fading + value_sums(count, heads, weights, value_win[start:])
        elif final:
            summed, total = summed_in[at], total_in[at]
        else:
            summed, top, total = summed_in[at], top_in[at], total_in[at]
        if final:
            out = (summed / jnp.sum(total, axis=1, keepdims=True)).astype(out_ref.dtype)
            out_ref[pl.ds(first, CHUNK)] = out.reshape(CHUNK, heads, depth)
            at = pl.ds(first, CHUNK)
            pltpu.make_async_copy(out_ref.at[at], out_to.at[at], left).start()
        else:
            for ref, value in zip(out_refs, (summed, top, total)):
                ref[at] = value

    column = lax.broadcasted_iota(jnp.int32, (1, window * BLOCK), 1)
    hidden = [jnp.where(column < (window - far) * BLOCK, lowest, 0.0) for far in fars]
    levels = sorted({0, min(2, window), window})
    even = window - window % 2
    cases = [(0, 0)] + [(n, m) for n in levels[1:] for m in sorted({0, 2, min(n, even)})]
    needed = [sum(jnp.where(far > low, high - low, 0) for low, high in zip(levels, levels[1:])) for far in fars]
    needed[1] = jnp.minimum(needed[1], even)
    for taking in cases:

        @pl.when(jnp.logical_and(needed[0] == taking[0], needed[1] == taking[1]))
        def _():
            in_chunks(blocks, functools.partial(work, taking))

    if final:
        pltpu.make_async_copy(out_ref, out_to, left).wait()


def body(queries, keys, values, doc_blocks):
    tokens, kv_heads, depth = keys.shape
    parts = lax.axis_size("kvh")
    count = kv_heads // parts
    rows, heads, _ = queries.shape
    sections = min(3, lax.axis_size("ctx") // 4)
    behind = 2**sections - 1
    per_shard = rows // BLOCK
    smem, vmem = pl.BlockSpec(memory_space=pltpu.SMEM), pl.BlockSpec(memory_space=pltpu.VMEM)
    params = pltpu.CompilerParams(vmem_limit_bytes=24 * 1024 * 1024)
    scale = 1.0 / math.sqrt(depth)
    light, medium = (
        pl.CostEstimate(flops=flops, bytes_accessed=2**20, transcendentals=10**6) for flops in (10**8, 10**9)
    )
    shape = jax.ShapeDtypeStruct
    me = lax.axis_index("kvh")
    index = (lax.axis_index("ctx") * parts + me).astype(jnp.int32).reshape(1)
    spans, last, nearer = pl.pallas_call(
        functools.partial(plan_kernel, parts, behind),
        cost_estimate=medium,
        out_shape=(shape((1,), jnp.int32), shape((1,), jnp.int32), shape((per_shard + 1, 8, 128), jnp.int32)),
        in_specs=[smem] * 2,
        out_specs=(smem, smem, vmem),
        name="plan",
    )(doc_blocks, index)
    both = lax.optimization_barrier(jnp.concatenate([keys, values], axis=2))
    both = both.reshape(tokens, parts, count, 2 * depth).transpose(1, 2, 0, 3)
    pieces = for_groups(both, me)
    swapped = passed_along(pieces[:, 1], 0, across=1)
    swapped, spans, last, nearer = lax.optimization_barrier((swapped, spans, last, nearer))
    here, there = (jnp.stack([pieces[side, 0], swapped[side]]) for side in range(2))
    own = [here, passed_along(there, 0, across=2)]
    far = [passed_along(here, 2), passed_along(there, 2, across=2)]
    one = [passed_along(here, 1), passed_along(there, 1, across=2)]
    for distance in range(3, behind):
        send = functools.partial(passed_along, by=distance)
        far += [lax.cond(spans[0] >= distance, send, lambda x: x, x) for x in own]

    own, one = lax.optimization_barrier((own, one))

    def late(parity):
        return lambda *halves: passed_along(jnp.where(me >= parts // 2, *halves), behind, parity=parity)

    far.append(lax.switch(last[0], [lambda *halves: halves[0], late(0), late(1), late(None)], *own))
    own, far[2:] = lax.optimization_barrier((own, far[2:]))

    state = [shape((rows * heads, depth), jnp.float32)] * 3

    def window(group):
        length = sum(s.shape[0] * s.shape[2] for s in group)
        return [
            pltpu.VMEM((count * depth, length), jnp.bfloat16),
            pltpu.VMEM((length, count * depth), jnp.bfloat16),
        ]

    kept = pl.pallas_call(
        functools.partial(own_kernel, scale),
        out_shape=state,
        in_specs=[vmem] * 4,
        out_specs=[vmem] * 3,
        scratch_shapes=window(own),
        compiler_params=params,
        cost_estimate=light,
        name="own",
    )(nearer, queries, *own)
    kept = pl.pallas_call(
        functools.partial(join_kernel, scale, 0, False),
        out_shape=state,
        in_specs=[vmem] * 7,
        out_specs=[vmem] * 3,
        scratch_shapes=window(one),
        compiler_params=params,
        cost_estimate=light,
        name="one",
    )(nearer, queries, *kept, *one)
    return pl.pallas_call(
        functools.partial(join_kernel, scale, per_shard, True),
        out_shape=shape(queries.shape, queries.dtype),
        in_specs=[vmem] * 7 + [pl.BlockSpec(memory_space=pl.ANY)] * (len(far) - 2),
        out_specs=pl.BlockSpec(memory_space=pl.ANY),
        scratch_shapes=[
            *window(far),
            pltpu.VMEM(queries.shape, queries.dtype),
            pltpu.SemaphoreType.DMA,
            pltpu.SemaphoreType.DMA((len(far) - 2,)),
            *[pltpu.VMEM(piece.shape, piece.dtype) for piece in far[2:]],
        ],
        compiler_params=params,
        cost_estimate=light,
        name="far",
    )(nearer, queries, *kept, *far)


def solution(mesh):
    in_specs = (
        P("ctx", "kvh", None),
        P(("ctx", "kvh"), None, None),
        P(("ctx", "kvh"), None, None),
        P(),
    )
    out_specs = P("ctx", "kvh", None)
    return jax.shard_map(body, mesh=mesh, in_specs=in_specs, out_specs=out_specs, check_vma=False)
```
